256 devices in a mesh: seq: 32 (over x, z), head: 8 (over y, core).
Axes of the slice: x: 4, y: 4, z: 8, core: 2. Of those that a mesh axis runs over, the one named last changes fastest.
Arguments:
- queries: bfloat16 [256, 64, 128], P('seq', 'head'), may hold values from -150 to 150, as said below
- prompt_keys: bfloat16 [131072, 8, 128], P('seq', 'head'), may hold values from -6 to 6
- prompt_values: bfloat16 [131072, 8, 128], P('seq', 'head'), may hold values from -6 to 6
- suffix_keys: bfloat16 [256, 512, 8, 128], P('seq', None, 'head'), may hold values from -9 to 9
- suffix_values: bfloat16 [256, 512, 8, 128], P('seq', None, 'head'), may hold values from -6 to 6
- new_keys: bfloat16 [256, 8, 128], P('seq', 'head'), may hold values from -9 to 9
- new_values: bfloat16 [256, 8, 128], P('seq', 'head'), may hold values from -6 to 6
- suffix_len: int32 [256], P('seq'), may hold values from 1 to 511, as said below
- ancestors: int32 [256], P('seq'), may hold values from 0 to 255, as said below
Outputs:
- attended: bfloat16 [256, 8192], P('seq', 'head')
- next_keys: bfloat16 [256, 512, 8, 128], P('seq', None, 'head')
- next_values: bfloat16 [256, 512, 8, 128], P('seq', None, 'head')
The draws below stay inside these ranges and needn't reach their ends.
Inputs may be any that keep to these rules, and one draw needn't show every extreme that they name: `queries`: queries are of order a few; the range is wide. `suffix_len`: at least one particle has generated exactly 511 tokens and one exactly 1. ancestors[q] differs from q by at most 4, and by exactly 4 for some q. In every aligned block of 8 particles, the first descends from a particle of the block below and the last from a particle of the block above, where such a block exists.
All inputs are finite; a program needn't handle non-finite values.
Results may differ from the reference program's by a relative error of at most 0.0024.
Values may be sent and summed in bfloat16 or wider, within the bound.
A program may use at most 192 MiB of HBM per device.

```python
import math
import jax
import jax.numpy as jnp
from jax import lax

HD = 128
QH = 64
KVH = 8
PART_DEV = 8
LEN_DEV = 4096
REACH = 4
PARTICLES = 256
PROMPT = 131072
SUFFIX = 512
N_SEQ = 32


def prompt_base(key):
    return jnp.clip(jax.random.normal(key, (LEN_DEV * N_SEQ, KVH, HD), jnp.float32), -6.0, 6.0)


def draw_prompt_keys(key, part):
    base = prompt_base(key)
    return base.astype(jnp.bfloat16)


def draw_queries(key, part):
    key = jax.random.fold_in(key, 2)
    values = 3.0 * jnp.clip(jax.random.normal(key, (PARTICLES, QH, HD), jnp.float32), -5.0, 5.0)
    return values.astype(jnp.bfloat16)


def draw_suffix_len(key, part):
    key = jax.random.fold_in(key, 3)
    lengths = jax.random.randint(key, (PARTICLES,), 1, SUFFIX)
    first = jax.random.randint(jax.random.fold_in(key, 1), (), 0, PARTICLES)
    second = (first + 1 + jax.random.randint(jax.random.fold_in(key, 2), (), 0, PARTICLES - 1)) % PARTICLES
    lengths = lengths.at[first].set(SUFFIX - 1)
    lengths = lengths.at[second].set(1)
    return lengths.astype(jnp.int32)


def draw_ancestors(key, part):
    key = jax.random.fold_in(key, 4)
    index = jnp.arange(PARTICLES, dtype=jnp.int32)
    offsets = jax.random.randint(key, (PARTICLES,), -REACH, REACH + 1)
    upward = jax.random.randint(jax.random.fold_in(key, 1), (PARTICLES,), 1, REACH + 1)
    downward = jax.random.randint(jax.random.fold_in(key, 2), (PARTICLES,), 1, REACH + 1)
    position = index % PART_DEV
    offsets = jnp.where(position == PART_DEV - 1, upward, offsets)
    offsets = jnp.where(position == 0, -downward, offsets)
    chosen = jnp.clip(index + offsets, 0, PARTICLES - 1)
    block_pick = jax.random.randint(jax.random.fold_in(key, 3), (), 1, PARTICLES // PART_DEV - 1)
    farthest = block_pick * PART_DEV + PART_DEV - 1
    chosen = chosen.at[farthest].set(farthest + REACH)
    return chosen.astype(jnp.int32)


def shard_levels(rng, extent, cuts, least, largest):
    level = 1.0
    for dim, blocks in cuts:
        steps = jax.random.uniform(jax.random.fold_in(jax.random.fold_in(rng, 6), dim), (blocks,), jnp.float32, least / len(cuts), largest / len(cuts))
        level = level * jnp.repeat(jnp.exp(steps), extent[dim] // blocks).reshape((-1,) + (1,) * (len(extent) - 1 - dim))
    return level


def centred(stream_key, extent, spread, limit, cuts=(), kind=jnp.bfloat16):
    values = spread * jax.random.normal(stream_key, extent, jnp.float32)
    if cuts:
        values = values * shard_levels(stream_key, extent, cuts, -0.22, 0.18)
    return jnp.clip(values, -limit, limit).astype(kind)


def setup_inputs(seed: int = 0) -> dict:
    arg_keys = jax.random.split(jax.random.key(seed), 10)
    queries = draw_queries(jax.random.fold_in(arg_keys[9], 71), 0)
    prompt_keys = draw_prompt_keys(jax.random.fold_in(arg_keys[9], 71), 0)
    prompt_values = centred(arg_keys[2], (PROMPT, KVH, HD), 1.0, 6.0, ((0, 32), (1, 8)))
    suffix_keys = centred(arg_keys[3], (PARTICLES, SUFFIX, KVH, HD), 1.5, 9.0, ((0, 32), (2, 8)))
    suffix_values = centred(arg_keys[4], (PARTICLES, SUFFIX, KVH, HD), 1.0, 6.0, ((0, 32), (2, 8)))
    new_keys = centred(arg_keys[5], (PARTICLES, KVH, HD), 1.5, 9.0, ((0, 32), (1, 8)))
    new_values = centred(arg_keys[6], (PARTICLES, KVH, HD), 1.0, 6.0, ((0, 32), (1, 8)))
    suffix_len = draw_suffix_len(jax.random.fold_in(arg_keys[9], 71), 0)
    ancestors = draw_ancestors(jax.random.fold_in(arg_keys[9], 71), 0)
    return {"queries": queries, "prompt_keys": prompt_keys, "prompt_values": prompt_values, "suffix_keys": suffix_keys, "suffix_values": suffix_values, "new_keys": new_keys, "new_values": new_values, "suffix_len": suffix_len, "ancestors": ancestors}


def reference(queries, prompt_keys, prompt_values, suffix_keys, suffix_values, new_keys, new_values, suffix_len, ancestors):
    group = QH // KVH
    score_scale = 1.0 / math.sqrt(HD)
    block = min(LEN_DEV, 2048)
    blocks_all = LEN_DEV * N_SEQ // block
    grouped = queries.reshape(PARTICLES, KVH, group, HD).transpose(1, 0, 2, 3)
    key_blocks = prompt_keys.reshape(blocks_all, block, KVH, HD).transpose(2, 0, 1, 3)
    value_blocks = prompt_values.reshape(blocks_all, block, KVH, HD).transpose(2, 0, 1, 3)
    suffix_k = suffix_keys.transpose(2, 0, 1, 3)
    suffix_v = suffix_values.transpose(2, 0, 1, 3)
    fresh_k = new_keys.transpose(1, 0, 2)
    fresh_v = new_values.transpose(1, 0, 2)
    slots = jnp.arange(SUFFIX, dtype=jnp.int32)
    live = slots[None, :] < suffix_len[:, None]

    def one_head(input_arrays):
        query_vector, local_key_rows, local_value_rows, suffix_key_rows, suffix_value_rows, noisy_key, noisy_value = input_arrays
        flat = query_vector.reshape(PARTICLES * group, HD)

        def visit(carry, pair):
            maxima, totals, weighted = carry
            block_of_keys, value_block = pair
            scores = jnp.dot(flat, block_of_keys.T, preferred_element_type=jnp.float32) * score_scale
            block_max = lax.optimization_barrier(jnp.max(scores, axis=1))
            weights = jnp.exp(scores - block_max[:, None])
            block_sum = lax.optimization_barrier(jnp.sum(weights, axis=1))
            block_out = jnp.dot(weights.astype(jnp.bfloat16), value_block, preferred_element_type=jnp.float32)
            merged = jnp.maximum(maxima, block_max)
            old_factor = jnp.exp(maxima - merged)
            new_factor = jnp.exp(block_max - merged)
            return ((merged, totals * old_factor + block_sum * new_factor, weighted * old_factor[:, None] + block_out * new_factor[:, None]), None)
        start = (jnp.full((PARTICLES * group,), -1e+30, jnp.float32), jnp.zeros((PARTICLES * group,), jnp.float32), jnp.zeros((PARTICLES * group, HD), jnp.float32))
        (prompt_max, prompt_sum, prompt_out), _ = lax.scan(visit, start, (local_key_rows, local_value_rows))
        prompt_max = prompt_max.reshape(PARTICLES, group)
        prompt_sum = prompt_sum.reshape(PARTICLES, group)
        prompt_out = prompt_out.reshape(PARTICLES, group, HD)
        query_vector32 = query_vector.astype(jnp.float32)
        suffix_score_rows = jnp.einsum('tku,tlu->tkl', query_vector32, suffix_key_rows.astype(jnp.float32)) * score_scale
        nscore = jnp.einsum('pgd,pd->pg', query_vector32, noisy_key.astype(jnp.float32)) * score_scale
        masked = jnp.where(live[:, None, :], suffix_score_rows, jnp.float32(-1e+30))
        suffix_max = jnp.maximum(lax.optimization_barrier(jnp.max(masked, axis=2)), nscore)
        sweights = jnp.where(live[:, None, :], jnp.exp(suffix_score_rows - suffix_max[..., None]), jnp.float32(0.0))
        nweight = jnp.exp(nscore - suffix_max)
        suffix_sum = lax.optimization_barrier(jnp.sum(sweights, axis=2)) + nweight
        srounded = lax.optimization_barrier(sweights.astype(jnp.bfloat16)).astype(jnp.float32)
        nrounded = lax.optimization_barrier(nweight.astype(jnp.bfloat16)).astype(jnp.float32)
        suffix_out = jnp.einsum('pgs,psd->pgd', srounded, suffix_value_rows.astype(jnp.float32))
        suffix_out = suffix_out + nrounded[..., None] * noisy_value.astype(jnp.float32)[:, None, :]
        top = jnp.maximum(prompt_max, suffix_max)
        first = jnp.exp(prompt_max - top)
        second = jnp.exp(suffix_max - top)
        denom = prompt_sum * first + suffix_sum * second
        return (prompt_out * first[..., None] + suffix_out * second[..., None]) / denom[..., None]
    heads_out = lax.map(one_head, (grouped, key_blocks, value_blocks, suffix_k, suffix_v, fresh_k, fresh_v))
    attended = heads_out.transpose(1, 0, 2, 3).reshape(PARTICLES, QH * HD).astype(jnp.bfloat16)
    here = slots[None, :] == suffix_len[:, None]
    zero = jnp.zeros((), jnp.bfloat16)
    updated_keys = jnp.where(here[:, :, None, None], new_keys[:, None], jnp.where(live[:, :, None, None], suffix_keys, zero))
    updated_values = jnp.where(here[:, :, None, None], new_values[:, None], jnp.where(live[:, :, None, None], suffix_values, zero))
    next_keys = jnp.take(updated_keys, ancestors, axis=0)
    next_values = jnp.take(updated_values, ancestors, axis=0)
    return (attended, next_keys, next_values)
```

```python
import functools
import math

import jax
import jax.numpy as jnp
from jax import lax
from jax.experimental import pallas as pl
from jax.experimental.pallas import tpu as pltpu
from jax.sharding import PartitionSpec as P

F32, BF16, I16, I32 = jnp.float32, jnp.bfloat16, jnp.int16, jnp.int32
MESH = pl.DeviceIdType.MESH
HD = 128
GROUP = 8
PART = 8
HALO = 4
ROWS = PART * GROUP
NX, NZ = 4, 8
TILE = 256
TILES = NX * NZ * ROWS // TILE
CHUNK = 512
LOG2E = math.log2(math.e)
SCALE = LOG2E / math.sqrt(HD)
CODE = 32000.0


def column(rows, j):
    return rows[:, j : j + 1]


def turned(parts):
    sub = lax.broadcasted_iota(I32, (16, HD), 0)
    top = jnp.zeros((16, HD), F32)
    for j, part in enumerate(parts):
        top = jnp.where(sub == j, part, top)
    return jnp.concatenate([top, jnp.zeros((HD - 16, HD), F32)], axis=0).T


def coded(values):
    largest = jnp.maximum(jnp.max(jnp.abs(values), axis=1, keepdims=True), 1e-30)
    codes = jnp.round(values * (CODE / largest)).astype(I32).astype(I16)
    return codes, largest


def attention_kernel(
    q_hbm,
    k_hbm,
    v_hbm,
    sk_hbm,
    sv_hbm,
    nk_ref,
    nv_ref,
    len_ref,
    att_ref,
    bk_hbm,
    bv_hbm,
    ak_hbm,
    av_hbm,
    bnew_ref,
    anew_ref,
    blen_ref,
    alen_ref,
    q_all,
    k_all,
    vx,
    sk,
    sv,
    new_own,
    len_own,
    s0,
    s1,
    m0,
    m1,
    acc,
    suf_o,
    suf_m,
    suf_l,
    own_o,
    own_st,
    xs_code,
    xs_st,
    xr_code,
    xr_st,
    zs_code,
    zs_st,
    zr_code,
    zr_st,
    out_rows,
    local_sem,
    agz_s,
    agz_r,
    agx_s,
    agx_r,
    rsx_s,
    rsx_r,
    rsz_s,
    rsz_r,
    halo_s,
    halo_r,
    small_s,
    small_r,
):
    me = lax.axis_index("seq")
    x, z = me // NZ, me % NZ
    owners = NX * NZ
    above, below = (me + 1) % owners, (me + owners - 1) % owners

    def z_peer(k):
        return x * NZ + (z + k) % NZ

    def x_peer(j):
        return ((x + j + j // 2 - 2 * (j // 3)) % NX) * NZ + z

    def back(j):
        return 3 - j + 3 * (j // 3)

    def remote(src, dst, send, recv, device):
        return pltpu.make_async_remote_copy(
            src, dst, send, recv, device_id={"seq": device}, device_id_type=MESH
        )

    partners = [z_peer(k) for k in range(1, NZ)] + [x_peer(j) for j in (1, 2, 3)] + [above, below]
    barrier = pltpu.get_barrier_semaphore()
    for p in partners:
        pl.semaphore_signal(barrier, inc=1, device_id={"seq": p}, device_id_type=MESH)

    def z_rows(zz):
        return pl.multiple_of(zz * ROWS + (zz // 4) * (TILES - 2) * TILE, ROWS)

    own_rows = pl.ds(z_rows(z), ROWS)
    locals_ = [
        pltpu.make_async_copy(q_hbm, q_all.at[own_rows], local_sem.at[0]),
        pltpu.make_async_copy(sk_hbm, sk, local_sem.at[1]),
        pltpu.make_async_copy(sv_hbm, sv, local_sem.at[2]),
        pltpu.make_async_copy(k_hbm, k_all, local_sem.at[3]),
        pltpu.make_async_copy(v_hbm, vx.at[:, pl.ds(0, HD)], local_sem.at[4]),
    ]
    for c in locals_:
        c.start()

    new_own[...] = jnp.concatenate(
        [nk_ref[...].astype(F32), nv_ref[...].astype(F32)], axis=0
    ).astype(BF16)
    sub = lax.broadcasted_iota(I32, (PART, HD), 0)
    lens = jnp.zeros((PART, HD), I32)
    for p in range(PART):
        lens = jnp.where(sub == p, len_ref[p], lens)
    len_own[...] = lens
    pl.semaphore_wait(barrier, len(partners))

    agz = [
        remote(q_hbm, q_all.at[own_rows], agz_s.at[k - 1], agz_r.at[NZ - 1 - k], z_peer(k))
        for k in range(1, NZ)
    ]
    agz_in = [
        remote(
            q_hbm,
            q_all.at[pl.ds(z_rows((z + k) % NZ), ROWS)],
            agz_s.at[k - 1],
            agz_r.at[k - 1],
            z_peer(k),
        )
        for k in range(1, NZ)
    ]
    for c in agz:
        c.start()

    small = [
        remote(new_own, bnew_ref, small_s.at[0], small_r.at[0], above),
        remote(new_own, anew_ref, small_s.at[1], small_r.at[1], below),
        remote(len_own, blen_ref, small_s.at[2], small_r.at[2], above),
        remote(len_own, alen_ref, small_s.at[3], small_r.at[3], below),
    ]
    for c in small:
        c.start()

    def halo(j):
        low, high = pl.ds(j, 1), pl.ds(j + PART - HALO, 1)
        return [
            remote(sk_hbm.at[high], bk_hbm.at[low], halo_s.at[j, 0], halo_r.at[j, 0], above),
            remote(sk_hbm.at[low], ak_hbm.at[low], halo_s.at[j, 1], halo_r.at[j, 1], below),
            remote(sv_hbm.at[high], bv_hbm.at[low], halo_s.at[j, 2], halo_r.at[j, 2], above),
            remote(sv_hbm.at[low], av_hbm.at[low], halo_s.at[j, 3], halo_r.at[j, 3], below),
        ]

    for c in halo(0):
        c.start()

    for c in locals_[:3]:
        c.wait()
    q_own = q_all[own_rows, :]
    q_own32 = q_own.astype(F32)
    nk32, nv32 = nk_ref[...].astype(F32), nv_ref[...].astype(F32)
    slot = lax.broadcasted_iota(I32, (GROUP, sk.shape[1]), 1)
    for p in range(PART):
        mine = slice(p * GROUP, (p + 1) * GROUP)
        s = lax.dot_general(q_own, sk[p], (((1,), (1,)), ((), ())), preferred_element_type=F32)
        s = s[mine] * SCALE
        new = jnp.sum(q_own32[mine] * nk32[p : p + 1], axis=1, keepdims=True) * SCALE
        live = slot < len_ref[p]
        top = jnp.maximum(jnp.max(jnp.where(live, s, -1e30), axis=1, keepdims=True), new)
        w = jnp.where(live, jnp.exp2(s - top), 0.0)
        nw = jnp.exp2(new - top)
        wide = jnp.concatenate([w, jnp.zeros_like(w)], axis=0).astype(BF16)
        o = jnp.dot(wide, sv[p], preferred_element_type=F32)[:GROUP]
        suf_o[mine, :] = o + nw.astype(BF16).astype(F32) * nv32[p : p + 1]
        suf_m[mine, :] = jnp.broadcast_to(top, (GROUP, HD))
        suf_l[mine, :] = jnp.broadcast_to(jnp.sum(w, axis=1, keepdims=True) + nw, (GROUP, HD))
    vx[:, HD:] = jnp.ones((vx.shape[0], HD), BF16)
    for c in locals_[3:]:
        c.wait()

    for c in agz_in:
        c.wait_recv()

    def agx(n, slot_there):
        half = n % 2
        src = q_all.at[pl.ds(half * (TILES - 1) * TILE, TILE)]
        dst = q_all.at[pl.ds(pl.multiple_of((1 + 2 * (slot_there - 1) + half) * TILE, TILE), TILE)]
        return src, dst

    def agx_out(n):
        j = n // 2 + 1
        src, dst = agx(n, back(j))
        return remote(src, dst, agx_s.at[n], agx_r.at[2 * (back(j) - 1) + n % 2], x_peer(j))

    def agx_in(n):
        j = n // 2 + 1
        src, dst = agx(n, j)
        return remote(src, dst, agx_s.at[n], agx_r.at[n], x_peer(j))

    for n in range(6):
        agx_out(n).start()

    def scores(t, keys):
        q = q_all[pl.ds(pl.multiple_of(t * TILE, TILE), TILE), :]
        return lax.dot_general(
            q, k_all[keys, :], (((1,), (1,)), ((), ())), preferred_element_type=F32
        )

    n_chunks = k_all.shape[0] // CHUNK

    def step(t, s_next, m_next, s_now, m_now):
        most = None
        for c in range(n_chunks):
            keys = slice(c * CHUNK, (c + 1) * CHUNK)
            if s_next is not None:
                s = scores(t + 1, keys)
                s_next[:, keys] = s
                for g in range(CHUNK // HD):
                    part = s[:, g * HD : (g + 1) * HD]
                    most = part if most is None else jnp.maximum(most, part)
            if s_now is not None:
                top = m_now[...]
                weights = [
                    jnp.exp2(s_now[:, lo : lo + HD] * SCALE - top).astype(BF16)
                    for lo in range(c * CHUNK, (c + 1) * CHUNK, HD)
                ]
                d = jnp.dot(
                    jnp.concatenate(weights, axis=1), vx[keys, :], preferred_element_type=F32
                )
                if c == 0:
                    acc[...] = d
                else:
                    acc[...] += d
        if s_next is not None:
            m_next[...] = jnp.broadcast_to(
                jnp.max(most, axis=1, keepdims=True) * SCALE, m_next.shape
            )

    lane = lax.broadcasted_iota(I32, (TILE, HD), 1)

    def normalised(m_now):
        total = acc[:, HD:]
        return acc[:, :HD] / total, m_now[...] + jnp.log(total) * LOG2E

    def put_stats(ref, lse, largest):
        both = jnp.where(lane == 0, lse, jnp.broadcast_to(largest, lse.shape))
        for g in range(TILE // HD):
            ref[g * 8 : (g + 1) * 8, :] = both[g * HD : (g + 1) * HD].T[:8]

    def rsx_copies(n, slot_there):
        i = 2 * (slot_there - 1) + n % 2
        j = n // 2 + 1
        return [
            remote(xs_code.at[n], xr_code.at[i], rsx_s.at[n, 0], rsx_r.at[i, 0], x_peer(j)),
            remote(xs_st.at[n], xr_st.at[i], rsx_s.at[n, 1], rsx_r.at[i, 1], x_peer(j)),
        ]

    def finish_peer(t, m_now):
        n = t - 1
        o, lse = normalised(m_now)
        codes, largest = coded(o)
        xs_code[n] = codes
        put_stats(xs_st.at[n], lse, largest)
        for c in rsx_copies(n, back(n // 2 + 1)):
            c.start()

    def finish_own(half, m_now):
        o, lse = normalised(m_now)
        own_o[half * TILE : (half + 1) * TILE, :] = o
        put_stats(own_st.at[half], lse, jnp.ones((TILE, 1), F32))

    step(-1, s0, m0, None, None)
    agx_in(0).wait_recv()
    step(0, s1, m1, s0, m0)
    finish_own(0, m0)

    def pair(i, _):
        t = 2 * i + 1
        for c in halo(i + 1):
            c.start()
        agx_in(t).wait_recv()
        step(t, s0, m0, s1, m1)
        finish_peer(t, m1)
        agx_in(t + 1).wait_recv()
        step(t + 1, s1, m1, s0, m0)
        finish_peer(t + 1, m0)
        return 0

    lax.fori_loop(0, 2, pair, 0)
    agx_in(5).wait_recv()
    step(5, s0, m0, s1, m1)
    finish_peer(5, m1)
    step(6, s1, m1, s0, m0)
    finish_peer(6, m0)
    step(7, None, None, s1, m1)
    finish_own(1, m1)

    def sum_x(half):
        for j in (1, 2, 3):
            n = 2 * (j - 1) + half
            for c in rsx_copies(n, j):
                c.wait_recv()
        for g in range(TILE // HD):
            rows = slice(g * HD, (g + 1) * HD)
            lse = [own_st[half, g * 8 : g * 8 + 1, :]]
            for j in range(3):
                lse.append(xr_st[2 * j + half, g * 8 : g * 8 + 1, :])
            top = functools.reduce(jnp.maximum, lse)
            w = [jnp.exp2(v - top) for v in lse]
            total = functools.reduce(jnp.add, w)
            factors = [w[0] / total]
            for j in range(3):
                largest = xr_st[2 * j + half, g * 8 + 1 : g * 8 + 2, :]
                factors.append(w[j + 1] / total * (largest * (1.0 / CODE)))
            cols = turned(factors)
            at = half * TILE + g * HD
            o = own_o[at : at + HD, :] * column(cols, 0)
            for j in range(3):
                codes = xr_code[2 * j + half, rows, :].astype(I32).astype(F32)
                o = o + codes * column(cols, j + 1)
            codes, largest = coded(o)
            zs_code[at : at + HD, :] = codes
            st = jnp.broadcast_to(largest, (HD, HD)).T[:8]
            sub8 = lax.broadcasted_iota(I32, (8, HD), 0)
            zs_st[at // HD] = jnp.where(sub8 == 0, top + jnp.log(total) * LOG2E, st)

    def z_copies(k, to_there):
        there = (z + k) % NZ
        src = there if to_there else z
        slot_ = z if to_there else there
        i = NZ - 1 - k if to_there else k - 1
        return [
            remote(
                zs_code.at[pl.ds(pl.multiple_of(there * ROWS, ROWS), ROWS)],
                zr_code.at[slot_],
                rsz_s.at[k - 1, 0],
                rsz_r.at[i, 0],
                z_peer(k),
            ),
            remote(zs_st.at[there // 2], zr_st.at[slot_], rsz_s.at[k - 1, 1], rsz_r.at[i, 1], z_peer(k)),
        ]

    sum_x(0)
    sum_x(1)
    for k in range(1, NZ):
        for c in z_copies(k, True):
            c.start()
    for c in halo(3):
        c.start()
    zr_code[z] = zs_code[pl.ds(pl.multiple_of(z * ROWS, ROWS), ROWS), :]
    zr_st[z] = zs_st[z // 2]
    for k in range(1, NZ):
        for c in z_copies(k, False):
            c.wait_recv()

    odd = z % 2 == 1
    lse, largest = [], []
    for i in range(NZ):
        st = zr_st[i]
        st = jnp.where(odd, pltpu.roll(st, HD // 2, 1), st)
        lse.append(st[0:1])
        largest.append(st[1:2])
    top = functools.reduce(jnp.maximum, lse)
    w = [jnp.exp2(v - top) for v in lse]
    total = functools.reduce(jnp.add, w)
    cols = turned([a * (b * (1.0 / CODE)) for a, b in zip(w, largest)] + [total, top])[:ROWS]
    o = jnp.zeros((ROWS, HD), F32)
    for i in range(NZ):
        o = o + zr_code[i].astype(I32).astype(F32) * column(cols, i)
    prompt_sum, prompt_max = column(cols, NZ), column(cols, NZ + 1)
    suffix_max = suf_m[...]
    both = jnp.maximum(prompt_max, suffix_max)
    first, second = jnp.exp2(prompt_max - both), jnp.exp2(suffix_max - both)
    denom = prompt_sum * first + suf_l[...] * second
    out_rows[...] = (o * first + suf_o[...] * second) / denom
    for h in range(GROUP):
        att_ref[:, h * HD : (h + 1) * HD] = out_rows[pl.ds(h, PART, stride=GROUP), :].astype(BF16)

    for c in agz:
        c.wait_send()
    for n in range(6):
        agx_out(n).wait_send()
        for c in rsx_copies(n, back(n // 2 + 1)):
            c.wait_send()
    for k in range(1, NZ):
        for c in z_copies(k, True):
            c.wait_send()
    for c in small:
        c.wait()
    for j in range(HALO):
        for c in halo(j):
            c.wait()


def resample_kernel(
    anc_ref,
    len_ref,
    blen_ref,
    alen_ref,
    nk_ref,
    nv_ref,
    bnew_ref,
    anew_ref,
    att_in,
    sk_hbm,
    sv_hbm,
    bk_hbm,
    bv_hbm,
    ak_hbm,
    av_hbm,
    att_ref,
    nk_hbm,
    nv_hbm,
    buf,
    fresh,
    in_sem,
    out_sem,
):
    first = lax.axis_index("seq") * PART
    slots = sk_hbm.shape[1]
    fresh[0:8, :] = nk_ref[...].astype(F32)
    fresh[8:16, :] = nv_ref[...].astype(F32)
    fresh[16:32, :] = bnew_ref[...].astype(F32)
    fresh[32:48, :] = anew_ref[...].astype(F32)
    att_ref[...] = att_in[...]

    def fetch(q, where, kind):
        local = anc_ref[q] - first
        own, low, high = (sk_hbm, bk_hbm, ak_hbm) if kind == 0 else (sv_hbm, bv_hbm, av_hbm)
        dst, sem = buf.at[2 * q + kind], in_sem.at[2 * q + kind]

        @pl.when(local < 0)
        def _():
            pltpu.make_async_copy(low.at[jnp.maximum(local + HALO, 0)], dst, sem).start()

        @pl.when(local >= PART)
        def _():
            pltpu.make_async_copy(
                high.at[jnp.minimum(jnp.maximum(local - PART, 0), HALO - 1)], dst, sem
            ).start()

        @pl.when(jnp.logical_and(local >= 0, local < PART))
        def _():
            pltpu.make_async_copy(
                own.at[jnp.minimum(jnp.maximum(local, 0), PART - 1)], dst, sem
            ).start()

    for q in range(PART):
        for kind in range(2):
            fetch(q, 0, kind)

    row = lax.broadcasted_iota(I32, (slots, HD), 0)
    for q in range(PART):
        local = anc_ref[q] - first
        is_low, is_high = local < 0, local >= PART
        at = jnp.where(is_low, local + PART, jnp.where(is_high, local - PART, local))
        at = jnp.minimum(jnp.maximum(at, 0), PART - 1)
        length = jnp.where(
            is_low, blen_ref[at, 0], jnp.where(is_high, alen_ref[at, 0], len_ref[at])
        )
        base = jnp.where(is_low, 16, jnp.where(is_high, 32, 0)) + at
        for kind in range(2):
            i = 2 * q + kind
            out = nk_hbm if kind == 0 else nv_hbm
            pltpu.make_async_copy(sk_hbm.at[0], buf.at[i], in_sem.at[i]).wait()
            fresh_row = fresh[pl.ds(base + kind * PART, 1), :]
            kept = jnp.where(row < length, buf[i].astype(F32), 0.0)
            buf[i] = jnp.where(row == length, fresh_row, kept).astype(BF16)
            pltpu.make_async_copy(buf.at[i], out.at[q], out_sem.at[i]).start()
    for q in range(PART):
        for kind in range(2):
            i = 2 * q + kind
            out = nk_hbm if kind == 0 else nv_hbm
            pltpu.make_async_copy(buf.at[i], out.at[q], out_sem.at[i]).wait()


def on_device(
    queries,
    prompt_keys,
    prompt_values,
    suffix_keys,
    suffix_values,
    new_keys,
    new_values,
    suffix_len,
    ancestors,
):
    slots, keys = suffix_keys.shape[1], prompt_keys.shape[0]
    q = queries.reshape(ROWS, HD)
    k, v = prompt_keys.reshape(keys, HD), prompt_values.reshape(keys, HD)
    sk, sv = suffix_keys.reshape(PART, slots, HD), suffix_values.reshape(PART, slots, HD)
    nk, nv = new_keys.reshape(PART, HD), new_values.reshape(PART, HD)
    any_, vmem, smem = (
        pl.BlockSpec(memory_space=pl.ANY),
        pl.BlockSpec(memory_space=pltpu.VMEM),
        pl.BlockSpec(memory_space=pltpu.SMEM),
    )
    shape = jax.ShapeDtypeStruct
    side = shape((HALO, slots, HD), BF16)
    dma = pltpu.SemaphoreType.DMA
    att, bk, bv, ak, av, bnew, anew, blen, alen = pl.pallas_call(
        attention_kernel,
        out_shape=(
            shape((PART, GROUP * HD), BF16),
            side,
            side,
            side,
            side,
            shape((2 * PART, HD), BF16),
            shape((2 * PART, HD), BF16),
            shape((PART, HD), I32),
            shape((PART, HD), I32),
        ),
        in_specs=[any_] * 5 + [vmem, vmem, smem],
        out_specs=(vmem, any_, any_, any_, any_, vmem, vmem, vmem, vmem),
        scratch_shapes=[
            pltpu.VMEM((TILES * TILE, HD), BF16),
            pltpu.VMEM((keys, HD), BF16),
            pltpu.VMEM((keys, 2 * HD), BF16),
            pltpu.VMEM((PART, slots, HD), BF16),
            pltpu.VMEM((PART, slots, HD), BF16),
            pltpu.VMEM((2 * PART, HD), BF16),
            pltpu.VMEM((PART, HD), I32),
            pltpu.VMEM((TILE, keys), F32),
            pltpu.VMEM((TILE, keys), F32),
            pltpu.VMEM((TILE, HD), F32),
            pltpu.VMEM((TILE, HD), F32),
            pltpu.VMEM((TILE, 2 * HD), F32),
            pltpu.VMEM((ROWS, HD), F32),
            pltpu.VMEM((ROWS, HD), F32),
            pltpu.VMEM((ROWS, HD), F32),
            pltpu.VMEM((2 * TILE, HD), F32),
            pltpu.VMEM((2, TILE // 16, HD), F32),
            pltpu.VMEM((6, TILE, HD), I16),
            pltpu.VMEM((6, TILE // 16, HD), F32),
            pltpu.VMEM((6, TILE, HD), I16),
            pltpu.VMEM((6, TILE // 16, HD), F32),
            pltpu.VMEM((2 * TILE, HD), I16),
            pltpu.VMEM((4, 8, HD), F32),
            pltpu.VMEM((NZ, ROWS, HD), I16),
            pltpu.VMEM((NZ, 8, HD), F32),
            pltpu.VMEM((ROWS, HD), F32),
            dma((5,)),
            dma((NZ - 1,)),
            dma((NZ - 1,)),
            dma((6,)),
            dma((6,)),
            dma((6, 2)),
            dma((6, 2)),
            dma((NZ - 1, 2)),
            dma((NZ - 1, 2)),
            dma((HALO, 4)),
            dma((HALO, 4)),
            dma((4,)),
            dma((4,)),
        ],
        compiler_params=pltpu.CompilerParams(
            collective_id=0, has_side_effects=True, vmem_limit_bytes=40 * 2**20
        ),
        name="attention",
    )(q, k, v, sk, sv, nk, nv, suffix_len)
    attended, next_keys, next_values = pl.pallas_call(
        resample_kernel,
        out_shape=(
            shape((PART, GROUP * HD), BF16),
            shape((PART, slots, HD), BF16),
            shape((PART, slots, HD), BF16),
        ),
        in_specs=[smem] * 4 + [vmem] * 5 + [any_] * 6,
        out_specs=(vmem, any_, any_),
        scratch_shapes=[
            pltpu.VMEM((2 * PART, slots, HD), BF16),
            pltpu.VMEM((6 * PART, HD), F32),
            dma((2 * PART,)),
            dma((2 * PART,)),
        ],
        compiler_params=pltpu.CompilerParams(vmem_limit_bytes=32 * 2**20),
        name="resample",
    )(ancestors, suffix_len, blen, alen, nk, nv, bnew, anew, att, sk, sv, bk, bv, ak, av)
    return (
        attended,
        next_keys.reshape(suffix_keys.shape),
        next_values.reshape(suffix_values.shape),
    )


def solution(mesh):
    in_specs = (
        P("seq", "head", None),
        P("seq", "head", None),
        P("seq", "head", None),
        P("seq", None, "head", None),
        P("seq", None, "head", None),
        P("seq", "head", None),
        P("seq", "head", None),
        P("seq"),
        P("seq"),
    )
    out_specs = (P("seq", "head"), P("seq", None, "head", None), P("seq", None, "head", None))
    return jax.shard_map(
        on_device, mesh=mesh, in_specs=in_specs, out_specs=out_specs, check_vma=False
    )
```

```python
import functools
import math

import jax
import jax.numpy as jnp
from jax import lax
from jax.experimental import pallas as pl
from jax.experimental.pallas import tpu as pltpu
from jax.sharding import PartitionSpec as P

F32, BF16, I16, I32 = jnp.float32, jnp.bfloat16, jnp.int16, jnp.int32
MESH = pl.DeviceIdType.MESH
HD = 128
GROUP = 8
PART = 8
HALO = 4
ROWS = PART * GROUP
NX, NZ = 4, 8
TILE = 256
TILES = NX * NZ * ROWS // TILE
CHUNK = 512
LOG2E = math.log2(math.e)
SCALE = LOG2E / math.sqrt(HD)
OFFSETS = (0, 1, 7, 2, 6, 3, 5, 4)
NEGATIVE = (0, 2, 1, 4, 3, 6, 5, 7)
CUT = 32
BUDGET = 42
PACKETS = 3
PACKET_AT = (-1, 1, 2)
VMEM_LIMIT = 60 * 2**20
CODE = 32000.0


def column(rows, j):
    return rows[:, j : j + 1]


def turned(parts):
    sub = lax.broadcasted_iota(I32, (16, HD), 0)
    top = jnp.zeros((16, HD), F32)
    for j, part in enumerate(parts):
        top = jnp.where(sub == j, part, top)
    return jnp.concatenate([top, jnp.zeros((HD - 16, HD), F32)], axis=0).T


def coded(values):
    largest = jnp.maximum(jnp.max(jnp.abs(values), axis=1, keepdims=True), 1e-30)
    codes = jnp.round(values * (CODE / largest)).astype(I32).astype(I16)
    return codes, largest


def attention_kernel(
    q_hbm,
    k_hbm,
    v_hbm,
    sk_hbm,
    sv_hbm,
    nk_hbm,
    nv_hbm,
    len_hbm,
    anc_hbm,
    att_ref,
    wk_hbm,
    wv_hbm,
    lowk_hbm,
    lowv_hbm,
    highk_hbm,
    highv_hbm,
    low_info,
    high_info,
    need_ref,
    q_all,
    k_all,
    vx,
    sk,
    sv,
    nk_ref,
    nv_ref,
    fresh,
    len_ref,
    anc_ref,
    info,
    low_at,
    high_at,
    to_above_k,
    to_above_v,
    to_below_k,
    to_below_v,
    s0,
    s1,
    m0,
    m1,
    acc,
    suf_o,
    suf_m,
    suf_l,
    own_o,
    own_st,
    xs_code,
    xs_st,
    xr_code,
    xr_st,
    zs_code,
    zs_st,
    zr_code,
    zr_st,
    out_rows,
    local_sem,
    win_sem,
    agz_s,
    agz_r,
    agx_s,
    agx_r,
    rsx_s,
    rsx_r,
    rsz_s,
    rsz_r,
    info_sem,
    info_s,
    info_r,
    halo_s,
    halo_r,
):
    me = lax.axis_index("seq")
    x, z = me // NZ, me % NZ
    owners = NX * NZ
    above, below = (me + 1) % owners, (me + owners - 1) % owners

    def z_peer(pos):
        return x * NZ + (z + OFFSETS[pos]) % NZ

    def x_peer(j):
        return ((x + j + j // 2 - 2 * (j // 3)) % NX) * NZ + z

    def back(j):
        return 3 - j + 3 * (j // 3)

    def remote(src, dst, send, recv, device):
        return pltpu.make_async_remote_copy(
            src, dst, send, recv, device_id={"seq": device}, device_id_type=MESH
        )

    partners = [z_peer(p) for p in range(1, NZ)] + [x_peer(j) for j in (1, 2, 3)] + [above, below]
    barrier = pltpu.get_barrier_semaphore()
    for p in partners:
        pl.semaphore_signal(barrier, inc=1, device_id={"seq": p}, device_id_type=MESH)

    def tile_of(j, half):
        return j if half == 0 else 4 + j % 3

    def own_rows(pos, count=1):
        return pl.ds((TILES - 1) * TILE * (pos // 4) + (pos % 4) * ROWS, count * ROWS)

    locals_ = [
        pltpu.make_async_copy(q_hbm, q_all.at[own_rows(0)], local_sem.at[0]),
        pltpu.make_async_copy(nk_hbm, nk_ref, local_sem.at[1]),
        pltpu.make_async_copy(nv_hbm, nv_ref, local_sem.at[2]),
        pltpu.make_async_copy(len_hbm, len_ref, local_sem.at[3]),
        pltpu.make_async_copy(sk_hbm, sk, local_sem.at[4]),
        pltpu.make_async_copy(sv_hbm, sv, local_sem.at[5]),
        pltpu.make_async_copy(k_hbm, k_all, local_sem.at[6]),
        pltpu.make_async_copy(v_hbm, vx.at[:, pl.ds(0, HD)], local_sem.at[7]),
        pltpu.make_async_copy(anc_hbm, anc_ref, local_sem.at[8]),
    ]
    for c in locals_:
        c.start()
    vx[:, HD:] = jnp.ones((vx.shape[0], HD), BF16)

    locals_[3].wait()
    locals_[8].wait()
    sub = lax.broadcasted_iota(I32, (PART, HD), 0)
    lane8 = lax.broadcasted_iota(I32, (PART, HD), 1)
    table = jnp.zeros((PART, HD), I32)
    for p in range(PART):
        table = jnp.where(sub == p, jnp.where(lane8 == 0, len_ref[p], anc_ref[p]), table)
    info[...] = table
    pl.semaphore_wait(barrier, len(partners))
    infos = [
        remote(info, low_info, info_s.at[0], info_r.at[0], above),
        remote(info, high_info, info_s.at[1], info_r.at[1], below),
    ]
    for c in infos:
        c.start()

    def agz_out(pos):
        return remote(
            q_hbm,
            q_all.at[own_rows(NEGATIVE[pos])],
            agz_s.at[pos - 1],
            agz_r.at[NEGATIVE[pos] - 1],
            z_peer(pos),
        )

    def agz_in(pos):
        return remote(
            q_hbm, q_all.at[own_rows(pos)], agz_s.at[pos - 1], agz_r.at[pos - 1], z_peer(pos)
        )

    parts = ((0, 1), (1, 3), (4, 4))

    def agx(part, j, slot_there):
        pos, count = parts[part]
        start = tile_of(slot_there, pos // 4) * TILE + (pos % 4) * ROWS
        src = q_hbm if part == 0 else q_all.at[own_rows(pos, count)]
        return src, q_all.at[pl.ds(start, count * ROWS)]

    def agx_out(part, j):
        src, dst = agx(part, j, back(j))
        return remote(src, dst, agx_s.at[part, j - 1], agx_r.at[part, back(j) - 1], x_peer(j))

    def agx_in(part, j):
        src, dst = agx(part, j, j)
        return remote(src, dst, agx_s.at[part, j - 1], agx_r.at[part, j - 1], x_peer(j))

    for pos in range(1, NZ):
        agz_out(pos).start()
    for j in (1, 2, 3):
        agx_out(0, j).start()

    for i in (0, 1, 2, 4, 5):
        locals_[i].wait()
    fresh[0:PART, :] = nk_ref[...].astype(F32)
    fresh[PART : 2 * PART, :] = nv_ref[...].astype(F32)
    pieces = sk.shape[0] // PART
    slots = pieces * CUT
    row = lax.broadcasted_iota(I32, (pieces, CUT, HD), 0) * CUT + lax.broadcasted_iota(
        I32, (pieces, CUT, HD), 1
    )

    def update(p):
        mine = slice(p * pieces, (p + 1) * pieces)
        for kind, cache in ((0, sk), (1, sv)):
            new = fresh[kind * PART + p : kind * PART + p + 1, :].reshape(1, 1, HD)
            kept = jnp.where(row < len_ref[p], cache[mine].astype(F32), 0.0)
            cache[mine] = jnp.where(row == len_ref[p], new, kept).astype(BF16)

    first = me * PART

    def starts(ancestors, lengths, base):
        at = [0]
        for j in range(HALO):
            wanted = functools.reduce(
                jnp.maximum, [jnp.where(ancestors(q) == base + j, 1, 0) for q in range(PART)]
            )
            at.append(at[-1] + wanted * (lengths(j) // CUT + 1))
        return at

    def pack(at, base, to_k, to_v):
        def body(i, _):
            j = sum(jnp.where(i >= at[n], 1, 0) for n in (1, 2, 3))
            begin = functools.reduce(
                jnp.maximum, [jnp.where(i >= at[n], at[n], 0) for n in (1, 2, 3)]
            )
            piece = (base + j) * pieces + jnp.minimum(i - begin, pieces - 1)
            to_k[i] = sk[piece]
            to_v[i] = sv[piece]
            return 0

        lax.fori_loop(0, BUDGET, body, 0, unroll=3)

    def packet(n):
        rows = pl.ds(n * (BUDGET // PACKETS), BUDGET // PACKETS)
        return [
            remote(src.at[rows], dst.at[rows], halo_s.at[n, i], halo_r.at[n, i], device)
            for i, (src, dst, device) in enumerate(
                (
                    (to_above_k, lowk_hbm, above),
                    (to_below_k, highk_hbm, below),
                    (to_above_v, lowv_hbm, above),
                    (to_below_v, highv_hbm, below),
                )
            )
        ]

    for pos in (1, 2, 3):
        agz_in(pos).wait_recv()
    for j in (1, 2, 3):
        agx_out(1, j).start()
    for p in range(PART):
        update(p)
    window = [
        pltpu.make_async_copy(sk, wk_hbm, win_sem.at[0]),
        pltpu.make_async_copy(sv, wv_hbm, win_sem.at[1]),
    ]
    for c in window:
        c.start()
    for c in infos:
        c.wait_recv()
    tables = [
        pltpu.make_async_copy(low_info, low_at, info_sem.at[0]),
        pltpu.make_async_copy(high_info, high_at, info_sem.at[1]),
    ]
    for c in tables:
        c.start()
    for c in tables:
        c.wait()
    pack(
        starts(lambda q: high_at[q, 1], lambda j: len_ref[PART - HALO + j], first + PART - HALO),
        PART - HALO,
        to_above_k,
        to_above_v,
    )
    pack(starts(lambda q: low_at[q, 1], lambda j: len_ref[j], first), 0, to_below_k, to_below_v)
    need = jnp.maximum(
        starts(lambda q: anc_ref[q], lambda j: low_at[PART - HALO + j, 0], first - HALO)[-1],
        starts(lambda q: anc_ref[q], lambda j: high_at[j, 0], first + PART)[-1],
    ).astype(F32)
    for n in range(PACKETS):
        if PACKET_AT[n] < 0:
            for c in packet(n):
                c.start()
    for pos in (4, 5, 6, 7):
        agz_in(pos).wait_recv()
    for j in (1, 2, 3):
        agx_out(2, j).start()
    for c in locals_[6:8]:
        c.wait()

    def scores(t, keys):
        q = q_all[pl.ds(pl.multiple_of(t * TILE, TILE), TILE), :]
        return lax.dot_general(
            q, k_all[keys, :], (((1,), (1,)), ((), ())), preferred_element_type=F32
        )

    n_chunks = k_all.shape[0] // CHUNK

    def step(t, s_next, m_next, s_now, m_now):
        most = None
        for c in range(n_chunks):
            keys = slice(c * CHUNK, (c + 1) * CHUNK)
            if s_next is not None:
                s = scores(t + 1, keys)
                s_next[:, keys] = s
                for g in range(CHUNK // HD):
                    part = s[:, g * HD : (g + 1) * HD]
                    most = part if most is None else jnp.maximum(most, part)
            if s_now is not None:
                top = m_now[...]
                weights = [
                    jnp.exp2(s_now[:, lo : lo + HD] * SCALE - top).astype(BF16)
                    for lo in range(c * CHUNK, (c + 1) * CHUNK, HD)
                ]
                d = jnp.dot(
                    jnp.concatenate(weights, axis=1), vx[keys, :], preferred_element_type=F32
                )
                if c == 0:
                    acc[...] = d
                else:
                    acc[...] += d
        if s_next is not None:
            m_next[...] = jnp.broadcast_to(
                jnp.max(most, axis=1, keepdims=True) * SCALE, m_next.shape
            )

    lane = lax.broadcasted_iota(I32, (TILE, HD), 1)

    def normalised(m_now):
        total = acc[:, HD:]
        return acc[:, :HD] / total, m_now[...] + jnp.log(total) * LOG2E

    def put_stats(ref, lse, largest):
        both = jnp.where(lane == 0, lse, jnp.broadcast_to(largest, lse.shape))
        for g in range(TILE // HD):
            st = both[g * HD : (g + 1) * HD].T[:8]
            ref[g * 8 : (g + 1) * 8, :] = jnp.where(sub == 2, need, st)

    def slot_of(n):
        return n + 1 - n // 3 * (4 - 3 * ((5 - n) // 2))

    def rsx_copies(n, i, j):
        return [
            remote(xs_code.at[n], xr_code.at[i], rsx_s.at[n, 0], rsx_r.at[i, 0], x_peer(j)),
            remote(xs_st.at[n], xr_st.at[i], rsx_s.at[n, 1], rsx_r.at[i, 1], x_peer(j)),
        ]

    def rsx_out(n):
        j = slot_of(n)
        half = n // 3
        return rsx_copies(n, 2 * (back(j) - 1) + half, j)

    def rsx_in(j, half):
        i = 2 * (j - 1) + half
        return rsx_copies(i, i, j)

    def finish_peer(t, m_now):
        n = t - 1
        o, lse = normalised(m_now)
        codes, largest = coded(o)
        xs_code[n] = codes
        put_stats(xs_st.at[n], lse, largest)
        for c in rsx_out(n):
            c.start()

    def finish_own(half, m_now):
        o, lse = normalised(m_now)
        own_o[half * TILE : (half + 1) * TILE, :] = o
        put_stats(own_st.at[half], lse, jnp.ones((TILE, 1), F32))

    def wait_tile(t):
        for n in range(6):
            j, half = (1, 2, 3, 3, 1, 2)[n], n // 3

            @pl.when(t == n + 1)
            def _():
                for part in (0, 1) if half == 0 else (2,):
                    agx_in(part, j).wait_recv()

    step(-1, s0, m0, None, None)

    def pair(i, _):
        t = 2 * i
        for n in range(PACKETS):

            @pl.when(i == PACKET_AT[n])
            def _():
                for c in packet(n):
                    c.start()

        wait_tile(t + 1)
        step(t, s1, m1, s0, m0)

        @pl.when(t == 0)
        def _():
            finish_own(0, m0)

        @pl.when(t > 0)
        def _():
            finish_peer(t, m0)

        wait_tile(t + 2)
        step(t + 1, s0, m0, s1, m1)
        finish_peer(t + 1, m1)
        return 0

    lax.fori_loop(0, 3, pair, 0)

    def sum_x(half):
        for j in (1, 2, 3):
            for c in rsx_in(j, half):
                c.wait_recv()
        for g in range(TILE // HD):
            rows = slice(g * HD, (g + 1) * HD)
            lse = [own_st[half, g * 8 : g * 8 + 1, :]]
            for j in range(3):
                lse.append(xr_st[2 * j + half, g * 8 : g * 8 + 1, :])
            top = functools.reduce(jnp.maximum, lse)
            w = [jnp.exp2(v - top) for v in lse]
            total = functools.reduce(jnp.add, w)
            factors = [w[0] / total]
            for j in range(3):
                largest = xr_st[2 * j + half, g * 8 + 1 : g * 8 + 2, :]
                factors.append(w[j + 1] / total * (largest * (1.0 / CODE)))
            cols = turned(factors)
            at = half * TILE + g * HD
            o = own_o[at : at + HD, :] * column(cols, 0)
            for j in range(3):
                codes = xr_code[2 * j + half, rows, :].astype(I32).astype(F32)
                o = o + codes * column(cols, j + 1)
            codes, largest = coded(o)
            zs_code[at : at + HD, :] = codes
            st = jnp.broadcast_to(largest, (HD, HD)).T[:8]
            sub8 = lax.broadcasted_iota(I32, (8, HD), 0)
            most = own_st[half, 2:3, :]
            for j in range(3):
                most = jnp.maximum(most, xr_st[2 * j + half, 2:3, :])
            st = jnp.where(sub8 == 2, most, st)
            zs_st[at // HD] = jnp.where(sub8 == 0, top + jnp.log(total) * LOG2E, st)

    def z_copies(pos, i):
        return [
            remote(
                zs_code.at[pl.ds(pos * ROWS, ROWS)],
                zr_code.at[i],
                rsz_s.at[pos - 1, 0],
                rsz_r.at[i - 1, 0],
                z_peer(pos),
            ),
            remote(
                zs_st.at[pos // 2], zr_st.at[i], rsz_s.at[pos - 1, 1], rsz_r.at[i - 1, 1], z_peer(pos)
            ),
        ]

    def z_out(pos):
        return z_copies(pos, NEGATIVE[pos])

    sum_x(0)
    for pos in (1, 2, 3):
        for c in z_out(pos):
            c.start()
    step(6, s1, m1, s0, m0)
    finish_peer(6, m0)
    step(7, None, None, s1, m1)
    finish_own(1, m1)
    sum_x(1)
    for pos in (4, 5, 6, 7):
        for c in z_out(pos):
            c.start()
    for n in range(PACKETS):
        if PACKET_AT[n] > 2:
            for c in packet(n):
                c.start()

    q_own = q_all[own_rows(0), :]
    q_own32 = q_own.astype(F32)
    slot = lax.broadcasted_iota(I32, (GROUP, slots), 1)
    for p in range(PART):
        mine = slice(p * GROUP, (p + 1) * GROUP)
        some = slice(p * pieces, (p + 1) * pieces)
        own_k, own_v = sk[some].reshape(slots, HD), sv[some].reshape(slots, HD)
        s = lax.dot_general(q_own, own_k, (((1,), (1,)), ((), ())), preferred_element_type=F32)
        s = s[mine] * SCALE
        new = jnp.sum(q_own32[mine] * fresh[p : p + 1, :], axis=1, keepdims=True) * SCALE
        live = slot < len_ref[p]
        top = jnp.maximum(jnp.max(jnp.where(live, s, -1e30), axis=1, keepdims=True), new)
        w = jnp.where(live, jnp.exp2(s - top), 0.0)
        nw = jnp.exp2(new - top)
        wide = jnp.concatenate([w, jnp.zeros_like(w)], axis=0).astype(BF16)
        o = jnp.dot(wide, own_v, preferred_element_type=F32)[:GROUP]
        suf_o[mine, :] = o + nw.astype(BF16).astype(F32) * fresh[PART + p : PART + p + 1, :]
        suf_m[mine, :] = jnp.broadcast_to(top, (GROUP, HD))
        suf_l[mine, :] = jnp.broadcast_to(jnp.sum(w, axis=1, keepdims=True) + nw, (GROUP, HD))

    zr_code[0] = zs_code[0:ROWS, :]
    zr_st[0] = zs_st[0]
    for pos in range(1, NZ):
        for c in z_copies(pos, pos):
            c.wait_recv()

    lse, largest = [], []
    need_ref[...] = functools.reduce(jnp.maximum, [zr_st[i] for i in range(NZ)])
    for i in range(NZ):
        st = zr_st[i]
        if NEGATIVE[i] % 2 == 1:
            st = pltpu.roll(st, HD // 2, 1)
        lse.append(st[0:1])
        largest.append(st[1:2])
    top = functools.reduce(jnp.maximum, lse)
    w = [jnp.exp2(v - top) for v in lse]
    total = functools.reduce(jnp.add, w)
    cols = turned([a * (b * (1.0 / CODE)) for a, b in zip(w, largest)] + [total, top])[:ROWS]
    o = jnp.zeros((ROWS, HD), F32)
    for i in range(NZ):
        o = o + zr_code[i].astype(I32).astype(F32) * column(cols, i)
    prompt_sum, prompt_max = column(cols, NZ), column(cols, NZ + 1)
    suffix_max = suf_m[...]
    both = jnp.maximum(prompt_max, suffix_max)
    first, second = jnp.exp2(prompt_max - both), jnp.exp2(suffix_max - both)
    denom = prompt_sum * first + suf_l[...] * second
    out_rows[...] = (o * first + suf_o[...] * second) / denom
    for h in range(GROUP):
        att_ref[:, h * HD : (h + 1) * HD] = out_rows[pl.ds(h, PART, stride=GROUP), :].astype(BF16)

    for pos in range(1, NZ):
        agz_out(pos).wait_send()
        for c in z_out(pos):
            c.wait_send()
    for j in (1, 2, 3):
        for part in range(3):
            agx_out(part, j).wait_send()
    for n in range(6):
        for c in rsx_out(n):
            c.wait_send()
    for c in window:
        c.wait()
    for c in infos:
        c.wait_send()
    for n in range(PACKETS):
        for c in packet(n):
            c.wait()


def halo_kernel(k_hbm, v_hbm, lowk, lowv, highk, highv, send, recv):
    me = lax.axis_index("seq")
    owners = NX * NZ
    above, below = (me + 1) % owners, (me + owners - 1) % owners
    pieces = k_hbm.shape[0] // PART
    barrier = pltpu.get_barrier_semaphore()
    for p in (above, below):
        pl.semaphore_signal(barrier, inc=1, device_id={"seq": p}, device_id_type=MESH)
    pl.semaphore_wait(barrier, 2)
    copies = [
        pltpu.make_async_remote_copy(
            src.at[pl.ds(at * pieces, HALO * pieces)],
            dst,
            send.at[i],
            recv.at[i],
            device_id={"seq": device},
            device_id_type=MESH,
        )
        for i, (src, at, dst, device) in enumerate(
            (
                (k_hbm, PART - HALO, lowk, above),
                (v_hbm, PART - HALO, lowv, above),
                (k_hbm, 0, highk, below),
                (v_hbm, 0, highv, below),
            )
        )
    ]
    for c in copies:
        c.start()
    for c in copies:
        c.wait()


def resample_kernel(
    packed,
    anc_ref,
    low_ref,
    high_ref,
    att_in,
    k_hbm,
    v_hbm,
    lowk,
    lowv,
    highk,
    highv,
    att_ref,
    nk_hbm,
    nv_hbm,
    buf,
    att_buf,
    in_sem,
    out_sem,
):
    first = lax.axis_index("seq") * PART
    slots = k_hbm.shape[0] * CUT // PART
    pieces = slots // CUT
    att = [
        pltpu.make_async_copy(att_in, att_buf, in_sem.at[2 * PART]),
        pltpu.make_async_copy(att_buf, att_ref, out_sem.at[2 * PART]),
    ]
    att[0].start()

    def places(base, lengths):
        row, out = 0, []
        for j in range(HALO):
            live = lengths(j) // CUT + 1
            out.append((row if packed else j * pieces, live))
            wanted = functools.reduce(
                jnp.maximum, [jnp.where(anc_ref[q] == base + j, 1, 0) for q in range(PART)]
            )
            row = row + wanted * live
        return out

    low = places(first - HALO, lambda j: low_ref[PART - HALO + j, 0])
    high = places(first + PART, lambda j: high_ref[j, 0])

    def pick(entries, j, which):
        value = entries[0][which]
        for n in range(1, HALO):
            value = jnp.where(j == n, entries[n][which], value)
        return value

    at = [anc_ref[q] - first for q in range(PART)]

    def fetch(q):
        local = at[q]

        def start(k, v):
            pltpu.make_async_copy(k, buf.at[2 * q], in_sem.at[2 * q]).start()
            pltpu.make_async_copy(v, buf.at[2 * q + 1], in_sem.at[2 * q + 1]).start()

        def side(entries, j, k, v):
            limit = k.shape[0] - pieces
            rows = pl.ds(jnp.minimum(jnp.maximum(pick(entries, j, 0), 0), limit), pieces)
            start(k.at[rows], v.at[rows])

        @pl.when(local < 0)
        def _():
            side(low, local + HALO, lowk, lowv)

        @pl.when(local >= PART)
        def _():
            side(high, local - PART, highk, highv)

        @pl.when(jnp.logical_and(local >= 0, local < PART))
        def _():
            own = jnp.minimum(jnp.maximum(local, 0), PART - 1)
            rows = pl.ds(own * pieces, pieces)
            start(k_hbm.at[rows], v_hbm.at[rows])

    for q in range(PART):
        fetch(q)
    row = lax.broadcasted_iota(I32, (pieces, CUT, HD), 0)
    for q in range(PART):
        local = at[q]
        for kind, out in ((0, nk_hbm), (1, nv_hbm)):
            i = 2 * q + kind
            pltpu.make_async_copy(k_hbm.at[pl.ds(0, pieces)], buf.at[i], in_sem.at[i]).wait()
            if packed:

                @pl.when(jnp.logical_or(local < 0, local >= PART))
                def _():
                    live = jnp.where(
                        local < 0, pick(low, local + HALO, 1), pick(high, local - PART, 1)
                    )
                    buf[i] = jnp.where(row < live, buf[i].astype(F32), 0.0).astype(BF16)

            pltpu.make_async_copy(buf.at[i], out.at[pl.ds(q * pieces, pieces)], out_sem.at[i]).start()
    att[0].wait()
    att[1].start()
    for q in range(PART):
        for kind, out in ((0, nk_hbm), (1, nv_hbm)):
            i = 2 * q + kind
            pltpu.make_async_copy(buf.at[i], out.at[pl.ds(q * pieces, pieces)], out_sem.at[i]).wait()
    att[1].wait()


def on_device(
    queries,
    prompt_keys,
    prompt_values,
    suffix_keys,
    suffix_values,
    new_keys,
    new_values,
    suffix_len,
    ancestors,
):
    slots, keys = suffix_keys.shape[1], prompt_keys.shape[0]
    q = queries.reshape(ROWS, HD)
    k, v = prompt_keys.reshape(keys, HD), prompt_values.reshape(keys, HD)
    sk = suffix_keys.reshape(PART * slots // CUT, CUT, HD)
    sv = suffix_values.reshape(PART * slots // CUT, CUT, HD)
    nk, nv = new_keys.reshape(PART, HD), new_values.reshape(PART, HD)
    hbm, vmem, smem = (
        pl.BlockSpec(memory_space=pltpu.HBM),
        pl.BlockSpec(memory_space=pltpu.VMEM),
        pl.BlockSpec(memory_space=pltpu.SMEM),
    )
    shape = jax.ShapeDtypeStruct
    window = shape((PART * slots // CUT, CUT, HD), BF16)
    side = shape((BUDGET + slots // CUT, CUT, HD), BF16)
    info = shape((PART, HD), I32)
    dma = pltpu.SemaphoreType.DMA
    att, wk, wv, lowk, lowv, highk, highv, low_info, high_info, need = pl.pallas_call(
        attention_kernel,
        out_shape=(
            shape((PART, GROUP * HD), BF16),
            window,
            window,
            side,
            side,
            side,
            side,
            info,
            info,
            shape((PART, HD), F32),
        ),
        in_specs=[hbm] * 9,
        out_specs=(vmem, hbm, hbm, hbm, hbm, hbm, hbm, vmem, vmem, vmem),
        scratch_shapes=[
            pltpu.VMEM((TILES * TILE, HD), BF16),
            pltpu.VMEM((keys, HD), BF16),
            pltpu.VMEM((keys, 2 * HD), BF16),
            pltpu.VMEM((PART * slots // CUT, CUT, HD), BF16),
            pltpu.VMEM((PART * slots // CUT, CUT, HD), BF16),
            pltpu.VMEM((PART, HD), BF16),
            pltpu.VMEM((PART, HD), BF16),
            pltpu.VMEM((2 * PART, HD), F32),
            pltpu.SMEM((PART,), I32),
            pltpu.SMEM((PART,), I32),
            pltpu.VMEM((PART, HD), I32),
            pltpu.SMEM((PART, HD), I32),
            pltpu.SMEM((PART, HD), I32),
            pltpu.VMEM((BUDGET, CUT, HD), BF16),
            pltpu.VMEM((BUDGET, CUT, HD), BF16),
            pltpu.VMEM((BUDGET, CUT, HD), BF16),
            pltpu.VMEM((BUDGET, CUT, HD), BF16),
            pltpu.VMEM((TILE, keys), F32),
            pltpu.VMEM((TILE, keys), F32),
            pltpu.VMEM((TILE, HD), F32),
            pltpu.VMEM((TILE, HD), F32),
            pltpu.VMEM((TILE, 2 * HD), F32),
            pltpu.VMEM((ROWS, HD), F32),
            pltpu.VMEM((ROWS, HD), F32),
            pltpu.VMEM((ROWS, HD), F32),
            pltpu.VMEM((2 * TILE, HD), F32),
            pltpu.VMEM((2, TILE // 16, HD), F32),
            pltpu.VMEM((6, TILE, HD), I16),
            pltpu.VMEM((6, TILE // 16, HD), F32),
            pltpu.VMEM((6, TILE, HD), I16),
            pltpu.VMEM((6, TILE // 16, HD), F32),
            pltpu.VMEM((2 * TILE, HD), I16),
            pltpu.VMEM((4, 8, HD), F32),
            pltpu.VMEM((NZ, ROWS, HD), I16),
            pltpu.VMEM((NZ, 8, HD), F32),
            pltpu.VMEM((ROWS, HD), F32),
            dma((9,)),
            dma((2,)),
            dma((NZ - 1,)),
            dma((NZ - 1,)),
            dma((3, 3)),
            dma((3, 3)),
            dma((6, 2)),
            dma((6, 2)),
            dma((NZ - 1, 2)),
            dma((NZ - 1, 2)),
            dma((2,)),
            dma((2,)),
            dma((2,)),
            dma((PACKETS, 4)),
            dma((PACKETS, 4)),
        ],
        compiler_params=pltpu.CompilerParams(
            collective_id=0, has_side_effects=True, vmem_limit_bytes=VMEM_LIMIT
        ),
        name="attention",
    )(q, k, v, sk, sv, nk, nv, suffix_len, ancestors)

    def resample(packed, *operands):
        return pl.pallas_call(
            functools.partial(resample_kernel, packed),
            out_shape=(
                shape((PART, GROUP * HD), BF16),
                window,
                window,
            ),
            in_specs=[smem, smem, smem] + [hbm] * 7,
            out_specs=(hbm, hbm, hbm),
            scratch_shapes=[
                pltpu.VMEM((2 * PART, slots // CUT, CUT, HD), BF16),
                pltpu.VMEM((PART, GROUP * HD), BF16),
                dma((2 * PART + 1,)),
                dma((2 * PART + 1,)),
            ],
            compiler_params=pltpu.CompilerParams(vmem_limit_bytes=VMEM_LIMIT),
            name="resample",
        )(*operands)

    def whole(anc, low_info, high_info, att, wk, wv, *_):
        full = shape((HALO * slots // CUT, CUT, HD), BF16)
        sides = pl.pallas_call(
            halo_kernel,
            out_shape=(full,) * 4,
            in_specs=[hbm] * 2,
            out_specs=(hbm,) * 4,
            scratch_shapes=[dma((4,)), dma((4,))],
            compiler_params=pltpu.CompilerParams(
                collective_id=1, has_side_effects=True, vmem_limit_bytes=VMEM_LIMIT
            ),
            name="halo",
        )(wk, wv)
        return resample(False, anc, low_info, high_info, att, wk, wv, *sides)

    attended, next_keys, next_values = lax.cond(
        need[2, 0] <= BUDGET,
        functools.partial(resample, True),
        whole,
        ancestors,
        low_info,
        high_info,
        att,
        wk,
        wv,
        lowk,
        lowv,
        highk,
        highv,
    )
    return (
        attended,
        next_keys.reshape(suffix_keys.shape),
        next_values.reshape(suffix_values.shape),
    )


def solution(mesh):
    in_specs = (
        P("seq", "head", None),
        P("seq", "head", None),
        P("seq", "head", None),
        P("seq", None, "head", None),
        P("seq", None, "head", None),
        P("seq", "head", None),
        P("seq", "head", None),
        P("seq"),
        P("seq"),
    )
    out_specs = (P("seq", "head"), P("seq", None, "head", None), P("seq", None, "head", None))
    return jax.shard_map(
        on_device, mesh=mesh, in_specs=in_specs, out_specs=out_specs, check_vma=False
    )
```

```python
import functools
import math

import jax
import jax.numpy as jnp
from jax import lax
from jax.experimental import pallas as pl
from jax.experimental.pallas import tpu as pltpu
from jax.sharding import PartitionSpec as P

F32, BF16, I16, I32 = jnp.float32, jnp.bfloat16, jnp.int16, jnp.int32
MESH = pl.DeviceIdType.MESH
HD = 128
GROUP = 8
PART = 8
HALO = 4
ROWS = PART * GROUP
NX, NZ = 4, 8
TILE = 256
TILES = NX * NZ * ROWS // TILE
CHUNK = 512
LOG2E = math.log2(math.e)
SCALE = LOG2E / math.sqrt(HD)
OFFSETS = (0, 1, 7, 2, 6, 3, 5, 4)
NEGATIVE = (0, 2, 1, 4, 3, 6, 5, 7)
CUT = 32
BUDGET = 44
CROSS = 34
PACKETS = 4
PACKET_AT = (-1, 0, 1, 2)
CROSS_AT = (1, 0, 2)
VMEM_LIMIT = 60 * 2**20
CODE = 32000.0


def column(rows, j):
    return rows[:, j : j + 1]


def turned(parts):
    sub = lax.broadcasted_iota(I32, (16, HD), 0)
    top = jnp.zeros((16, HD), F32)
    for j, part in enumerate(parts):
        top = jnp.where(sub == j, part, top)
    return jnp.concatenate([top, jnp.zeros((HD - 16, HD), F32)], axis=0).T


def coded(values):
    largest = jnp.maximum(jnp.max(jnp.abs(values), axis=1, keepdims=True), 1e-30)
    codes = jnp.round(values * (CODE / largest)).astype(I32).astype(I16)
    return codes, largest


def attention_kernel(
    q_hbm,
    k_hbm,
    v_hbm,
    sk_hbm,
    sv_hbm,
    nk_hbm,
    nv_hbm,
    len_hbm,
    anc_hbm,
    att_ref,
    wk_hbm,
    wv_hbm,
    lowk_hbm,
    lowv_hbm,
    highk_hbm,
    highv_hbm,
    plan_ref,
    fits_ref,
    q_all,
    k_all,
    vx,
    sk,
    sv,
    nk_ref,
    nv_ref,
    fresh,
    len_ref,
    anc_ref,
    info,
    low_info,
    high_info,
    low_at,
    high_at,
    to_above_k,
    to_above_v,
    to_below_k,
    to_below_v,
    relay_k,
    relay_v,
    s0,
    s1,
    m0,
    m1,
    acc,
    suf_o,
    suf_m,
    suf_l,
    own_o,
    own_st,
    xs_code,
    xs_st,
    xr_code,
    xr_st,
    zs_code,
    zs_st,
    zr_code,
    zr_st,
    out_rows,
    local_sem,
    win_sem,
    agz_s,
    agz_r,
    agx_s,
    agx_r,
    rsx_s,
    rsx_r,
    rsz_s,
    rsz_r,
    info_sem,
    info_s,
    info_r,
    halo_s,
    halo_r,
    cross_s,
    cross_r,
):
    me = lax.axis_index("seq")
    x, z = me // NZ, me % NZ
    owners = NX * NZ
    above, below = (me + 1) % owners, (me + owners - 1) % owners

    def z_peer(pos):
        return x * NZ + (z + OFFSETS[pos]) % NZ

    def x_peer(j):
        return ((x + j + j // 2 - 2 * (j // 3)) % NX) * NZ + z

    def back(j):
        return 3 - j + 3 * (j // 3)

    def remote(src, dst, send, recv, device):
        return pltpu.make_async_remote_copy(
            src, dst, send, recv, device_id={"seq": device}, device_id_type=MESH
        )

    partners = [z_peer(p) for p in range(1, NZ)] + [x_peer(j) for j in (1, 2, 3)] + [above, below]
    barrier = pltpu.get_barrier_semaphore()
    for p in partners:
        pl.semaphore_signal(barrier, inc=1, device_id={"seq": p}, device_id_type=MESH)

    def tile_of(j, half):
        return j if half == 0 else 4 + j % 3

    def own_rows(pos, count=1):
        return pl.ds((TILES - 1) * TILE * (pos // 4) + (pos % 4) * ROWS, count * ROWS)

    locals_ = [
        pltpu.make_async_copy(q_hbm, q_all.at[own_rows(0)], local_sem.at[0]),
        pltpu.make_async_copy(nk_hbm, nk_ref, local_sem.at[1]),
        pltpu.make_async_copy(nv_hbm, nv_ref, local_sem.at[2]),
        pltpu.make_async_copy(len_hbm, len_ref, local_sem.at[3]),
        pltpu.make_async_copy(sk_hbm, sk, local_sem.at[4]),
        pltpu.make_async_copy(sv_hbm, sv, local_sem.at[5]),
        pltpu.make_async_copy(k_hbm, k_all, local_sem.at[6]),
        pltpu.make_async_copy(v_hbm, vx.at[:, pl.ds(0, HD)], local_sem.at[7]),
        pltpu.make_async_copy(anc_hbm, anc_ref, local_sem.at[8]),
    ]
    for c in locals_:
        c.start()
    vx[:, HD:] = jnp.ones((vx.shape[0], HD), BF16)

    locals_[3].wait()
    locals_[8].wait()
    sub = lax.broadcasted_iota(I32, (PART, HD), 0)
    lane8 = lax.broadcasted_iota(I32, (PART, HD), 1)
    table = jnp.zeros((PART, HD), I32)
    for p in range(PART):
        table = jnp.where(sub == p, jnp.where(lane8 == 0, len_ref[p], anc_ref[p]), table)
    info[...] = table
    pl.semaphore_wait(barrier, len(partners))
    infos = [
        remote(info, low_info, info_s.at[0], info_r.at[0], above),
        remote(info, high_info, info_s.at[1], info_r.at[1], below),
    ]
    for c in infos:
        c.start()

    def agz_out(pos):
        return remote(
            q_hbm,
            q_all.at[own_rows(NEGATIVE[pos])],
            agz_s.at[pos - 1],
            agz_r.at[NEGATIVE[pos] - 1],
            z_peer(pos),
        )

    def agz_in(pos):
        return remote(
            q_hbm, q_all.at[own_rows(pos)], agz_s.at[pos - 1], agz_r.at[pos - 1], z_peer(pos)
        )

    parts = ((0, 1), (1, 3), (4, 4))

    def agx(part, j, slot_there):
        pos, count = parts[part]
        start = tile_of(slot_there, pos // 4) * TILE + (pos % 4) * ROWS
        src = q_hbm if part == 0 else q_all.at[own_rows(pos, count)]
        return src, q_all.at[pl.ds(start, count * ROWS)]

    def agx_out(part, j):
        src, dst = agx(part, j, back(j))
        return remote(src, dst, agx_s.at[part, j - 1], agx_r.at[part, back(j) - 1], x_peer(j))

    def agx_in(part, j):
        src, dst = agx(part, j, j)
        return remote(src, dst, agx_s.at[part, j - 1], agx_r.at[part, j - 1], x_peer(j))

    for pos in range(1, NZ):
        agz_out(pos).start()
    for j in (1, 2, 3):
        agx_out(0, j).start()

    for i in (0, 1, 2, 4, 5):
        locals_[i].wait()
    fresh[0:PART, :] = nk_ref[...].astype(F32)
    fresh[PART : 2 * PART, :] = nv_ref[...].astype(F32)
    pieces = sk.shape[0] // PART
    slots = pieces * CUT
    row = lax.broadcasted_iota(I32, (pieces, CUT, HD), 0) * CUT + lax.broadcasted_iota(
        I32, (pieces, CUT, HD), 1
    )

    def update(p):
        mine = slice(p * pieces, (p + 1) * pieces)
        for kind, cache in ((0, sk), (1, sv)):
            new = fresh[kind * PART + p : kind * PART + p + 1, :].reshape(1, 1, HD)
            kept = jnp.where(row < len_ref[p], cache[mine].astype(F32), 0.0)
            cache[mine] = jnp.where(row == len_ref[p], new, kept).astype(BF16)

    first = me * PART

    def starts(ancestors, lengths, base):
        at = [0]
        for j in range(HALO):
            wanted = functools.reduce(
                jnp.maximum, [jnp.where(ancestors(q) == base + j, 1, 0) for q in range(PART)]
            )
            at.append(at[-1] + wanted * (lengths(j) // CUT + 1))
        return at

    def pack(at, base, to_k, to_v):
        def body(i, _):
            j = sum(jnp.where(i >= at[n], 1, 0) for n in (1, 2, 3))
            begin = functools.reduce(
                jnp.maximum, [jnp.where(i >= at[n], at[n], 0) for n in (1, 2, 3)]
            )
            piece = (base + j) * pieces + jnp.minimum(i - begin, pieces - 1)
            to_k[i] = sk[piece]
            to_v[i] = sv[piece]
            return 0

        lax.fori_loop(0, BUDGET, body, 0, unroll=4)

    to_above, to_below = (to_above_k, to_above_v), (to_below_k, to_below_v)
    low, high = (lowk_hbm, lowv_hbm), (highk_hbm, highv_hbm)
    at_top, at_bottom = z == NZ - 1, z == 0

    def packet(n, up):
        rows = pl.ds(n * (BUDGET // PACKETS), BUDGET // PACKETS)
        src, dst, device = (to_above, low, above) if up else (to_below, high, below)
        i = 0 if up else 2
        return [
            remote(
                src[kind].at[rows],
                dst[kind].at[rows],
                halo_s.at[n, i + kind],
                halo_r.at[n, i + kind],
                device,
            )
            for kind in range(2)
        ]

    def cross(stage, up):
        src, dst, device = (to_above, low, above) if up else (to_below, high, below)
        near, far = pl.ds(0, CROSS // 2), pl.ds(CROSS // 2, CROSS // 2)
        relay = (relay_k, relay_v)
        along = 1 if up else 2
        out = []
        for kind in range(2):
            if stage == 0:
                ends = src[kind].at[near], dst[kind].at[near], device
            elif stage == 1:
                ends = src[kind].at[far], relay[kind], x_peer(along)
            else:
                ends = relay[kind], dst[kind].at[far], z_peer(along)
            a, b, there = ends
            out.append(remote(a, b, cross_s.at[stage, kind], cross_r.at[stage, kind], there))
        return out

    def send_halo(when):
        for n in range(PACKETS):
            for up, edge in ((True, at_top), (False, at_bottom)):

                @pl.when(jnp.logical_and(when == PACKET_AT[n], jnp.logical_not(edge)))
                def _():
                    for c in packet(n, up):
                        c.start()

        for stage in range(3):
            for up, edge in ((True, at_top), (False, at_bottom)):

                @pl.when(jnp.logical_and(when == CROSS_AT[stage], edge))
                def _():
                    if stage == 2:
                        for c in cross(1, up):
                            c.wait_recv()
                    for c in cross(stage, up):
                        c.start()

    def finish_halo():
        for up, edge in ((True, at_top), (False, at_bottom)):

            @pl.when(jnp.logical_not(edge))
            def _():
                for n in range(PACKETS):
                    for c in packet(n, up):
                        c.wait_send()
                    for c in packet(n, not up):
                        c.wait_recv()

            @pl.when(edge)
            def _():
                for stage in range(3):
                    for c in cross(stage, up):
                        c.wait_send()
                for stage in (0, 2):
                    for c in cross(stage, not up):
                        c.wait_recv()

    for pos in (1, 2, 3):
        agz_in(pos).wait_recv()
    for j in (1, 2, 3):
        agx_out(1, j).start()
    for p in range(PART):
        update(p)
    window = [
        pltpu.make_async_copy(sk, wk_hbm, win_sem.at[0]),
        pltpu.make_async_copy(sv, wv_hbm, win_sem.at[1]),
    ]
    for c in window:
        c.start()
    for c in infos:
        c.wait_recv()
    tables = [
        pltpu.make_async_copy(low_info, low_at, info_sem.at[0]),
        pltpu.make_async_copy(high_info, high_at, info_sem.at[1]),
    ]
    for c in tables:
        c.start()
    for c in tables:
        c.wait()
    pack(
        starts(lambda q: high_at[q, 1], lambda j: len_ref[PART - HALO + j], first + PART - HALO),
        PART - HALO,
        to_above_k,
        to_above_v,
    )
    pack(starts(lambda q: low_at[q, 1], lambda j: len_ref[j], first), 0, to_below_k, to_below_v)
    extra = BUDGET - CROSS
    low_row = starts(lambda q: anc_ref[q], lambda j: low_at[PART - HALO + j, 0], first - HALO)
    high_row = starts(lambda q: anc_ref[q], lambda j: high_at[j, 0], first + PART)
    need = jnp.maximum(
        low_row[-1] + jnp.where(at_bottom, extra, 0), high_row[-1] + jnp.where(at_top, extra, 0)
    ).astype(F32)

    for q in range(PART):
        local = anc_ref[q] - first
        is_low, is_high = local < 0, local >= PART
        place = jnp.where(is_low, local + HALO, jnp.where(is_high, local - PART, local))
        begin, live = local * pieces, pieces
        for j in range(HALO):
            chosen = jnp.logical_and(is_low, place == j)
            begin = jnp.where(chosen, low_row[j], begin)
            live = jnp.where(chosen, low_at[PART - HALO + j, 0] // CUT + 1, live)
            chosen = jnp.logical_and(is_high, place == j)
            begin = jnp.where(chosen, high_row[j], begin)
            live = jnp.where(chosen, high_at[j, 0] // CUT + 1, live)
        plan_ref[q] = jnp.where(is_low, 1, jnp.where(is_high, 2, 0))
        plan_ref[PART + q] = place
        plan_ref[2 * PART + q] = begin
        plan_ref[3 * PART + q] = live
    send_halo(-1)
    for pos in (4, 5, 6, 7):
        agz_in(pos).wait_recv()
    for j in (1, 2, 3):
        agx_out(2, j).start()
    for c in locals_[6:8]:
        c.wait()

    def scores(t, keys):
        q = q_all[pl.ds(pl.multiple_of(t * TILE, TILE), TILE), :]
        return lax.dot_general(
            q, k_all[keys, :], (((1,), (1,)), ((), ())), preferred_element_type=F32
        )

    n_chunks = k_all.shape[0] // CHUNK

    def step(t, s_next, m_next, s_now, m_now):
        most = None
        for c in range(n_chunks):
            keys = slice(c * CHUNK, (c + 1) * CHUNK)
            if s_next is not None:
                s = scores(t + 1, keys)
                s_next[:, keys] = s
                for g in range(CHUNK // HD):
                    part = s[:, g * HD : (g + 1) * HD]
                    most = part if most is None else jnp.maximum(most, part)
            if s_now is not None:
                top = m_now[...]
                weights = [
                    jnp.exp2(s_now[:, lo : lo + HD] * SCALE - top).astype(BF16)
                    for lo in range(c * CHUNK, (c + 1) * CHUNK, HD)
                ]
                d = jnp.dot(
                    jnp.concatenate(weights, axis=1), vx[keys, :], preferred_element_type=F32
                )
                if c == 0:
                    acc[...] = d
                else:
                    acc[...] += d
        if s_next is not None:
            m_next[...] = jnp.broadcast_to(
                jnp.max(most, axis=1, keepdims=True) * SCALE, m_next.shape
            )

    lane = lax.broadcasted_iota(I32, (TILE, HD), 1)

    def normalised(m_now):
        total = acc[:, HD:]
        return acc[:, :HD] / total, m_now[...] + jnp.log(total) * LOG2E

    def put_stats(ref, lse, largest):
        both = jnp.where(lane == 0, lse, jnp.broadcast_to(largest, lse.shape))
        for g in range(TILE // HD):
            st = both[g * HD : (g + 1) * HD].T[:8]
            ref[g * 8 : (g + 1) * 8, :] = jnp.where(sub == 2, need, st)

    def slot_of(n):
        return n + 1 - n // 3 * (4 - 3 * ((5 - n) // 2))

    def rsx_copies(n, i, j):
        return [
            remote(xs_code.at[n], xr_code.at[i], rsx_s.at[n, 0], rsx_r.at[i, 0], x_peer(j)),
            remote(xs_st.at[n], xr_st.at[i], rsx_s.at[n, 1], rsx_r.at[i, 1], x_peer(j)),
        ]

    def rsx_out(n):
        j = slot_of(n)
        half = n // 3
        return rsx_copies(n, 2 * (back(j) - 1) + half, j)

    def rsx_in(j, half):
        i = 2 * (j - 1) + half
        return rsx_copies(i, i, j)

    def finish_peer(t, m_now):
        n = t - 1
        o, lse = normalised(m_now)
        codes, largest = coded(o)
        xs_code[n] = codes
        put_stats(xs_st.at[n], lse, largest)
        for c in rsx_out(n):
            c.start()

    def finish_own(half, m_now):
        o, lse = normalised(m_now)
        own_o[half * TILE : (half + 1) * TILE, :] = o
        put_stats(own_st.at[half], lse, jnp.ones((TILE, 1), F32))

    def wait_tile(t):
        for n in range(6):
            j, half = (1, 2, 3, 3, 1, 2)[n], n // 3

            @pl.when(t == n + 1)
            def _():
                for part in (0, 1) if half == 0 else (2,):
                    agx_in(part, j).wait_recv()

    step(-1, s0, m0, None, None)

    def pair(i, _):
        t = 2 * i
        send_halo(i)
        wait_tile(t + 1)
        step(t, s1, m1, s0, m0)

        @pl.when(t == 0)
        def _():
            finish_own(0, m0)

        @pl.when(t > 0)
        def _():
            finish_peer(t, m0)

        wait_tile(t + 2)
        step(t + 1, s0, m0, s1, m1)
        finish_peer(t + 1, m1)
        return 0

    lax.fori_loop(0, 3, pair, 0)

    def sum_x(half):
        for j in (1, 2, 3):
            for c in rsx_in(j, half):
                c.wait_recv()
        for g in range(TILE // HD):
            rows = slice(g * HD, (g + 1) * HD)
            lse = [own_st[half, g * 8 : g * 8 + 1, :]]
            for j in range(3):
                lse.append(xr_st[2 * j + half, g * 8 : g * 8 + 1, :])
            top = functools.reduce(jnp.maximum, lse)
            w = [jnp.exp2(v - top) for v in lse]
            total = functools.reduce(jnp.add, w)
            factors = [w[0] / total]
            for j in range(3):
                largest = xr_st[2 * j + half, g * 8 + 1 : g * 8 + 2, :]
                factors.append(w[j + 1] / total * (largest * (1.0 / CODE)))
            cols = turned(factors)
            at = half * TILE + g * HD
            o = own_o[at : at + HD, :] * column(cols, 0)
            for j in range(3):
                codes = xr_code[2 * j + half, rows, :].astype(I32).astype(F32)
                o = o + codes * column(cols, j + 1)
            codes, largest = coded(o)
            zs_code[at : at + HD, :] = codes
            st = jnp.broadcast_to(largest, (HD, HD)).T[:8]
            sub8 = lax.broadcasted_iota(I32, (8, HD), 0)
            most = own_st[half, 2:3, :]
            for j in range(3):
                most = jnp.maximum(most, xr_st[2 * j + half, 2:3, :])
            st = jnp.where(sub8 == 2, most, st)
            zs_st[at // HD] = jnp.where(sub8 == 0, top + jnp.log(total) * LOG2E, st)

    def z_copies(pos, i):
        return [
            remote(
                zs_code.at[pl.ds(pos * ROWS, ROWS)],
                zr_code.at[i],
                rsz_s.at[pos - 1, 0],
                rsz_r.at[i - 1, 0],
                z_peer(pos),
            ),
            remote(
                zs_st.at[pos // 2], zr_st.at[i], rsz_s.at[pos - 1, 1], rsz_r.at[i - 1, 1], z_peer(pos)
            ),
        ]

    def z_out(pos):
        return z_copies(pos, NEGATIVE[pos])

    sum_x(0)
    for pos in (1, 2, 3):
        for c in z_out(pos):
            c.start()
    step(6, s1, m1, s0, m0)
    finish_peer(6, m0)
    step(7, None, None, s1, m1)
    finish_own(1, m1)
    sum_x(1)
    for pos in (4, 5, 6, 7):
        for c in z_out(pos):
            c.start()
    send_halo(3)

    q_own = q_all[own_rows(0), :]
    q_own32 = q_own.astype(F32)
    slot = lax.broadcasted_iota(I32, (GROUP, slots), 1)
    for p in range(PART):
        mine = slice(p * GROUP, (p + 1) * GROUP)
        some = slice(p * pieces, (p + 1) * pieces)
        own_k, own_v = sk[some].reshape(slots, HD), sv[some].reshape(slots, HD)
        s = lax.dot_general(q_own, own_k, (((1,), (1,)), ((), ())), preferred_element_type=F32)
        s = s[mine] * SCALE
        new = jnp.sum(q_own32[mine] * fresh[p : p + 1, :], axis=1, keepdims=True) * SCALE
        live = slot < len_ref[p]
        top = jnp.maximum(jnp.max(jnp.where(live, s, -1e30), axis=1, keepdims=True), new)
        w = jnp.where(live, jnp.exp2(s - top), 0.0)
        nw = jnp.exp2(new - top)
        wide = jnp.concatenate([w, jnp.zeros_like(w)], axis=0).astype(BF16)
        o = jnp.dot(wide, own_v, preferred_element_type=F32)[:GROUP]
        suf_o[mine, :] = o + nw.astype(BF16).astype(F32) * fresh[PART + p : PART + p + 1, :]
        suf_m[mine, :] = jnp.broadcast_to(top, (GROUP, HD))
        suf_l[mine, :] = jnp.broadcast_to(jnp.sum(w, axis=1, keepdims=True) + nw, (GROUP, HD))

    zr_code[0] = zs_code[0:ROWS, :]
    zr_st[0] = zs_st[0]
    for pos in range(1, NZ):
        for c in z_copies(pos, pos):
            c.wait_recv()

    lse, largest = [], []
    most = jnp.max(functools.reduce(jnp.maximum, [zr_st[i][2:3] for i in range(NZ)]))
    fits_ref[0] = jnp.where(most <= BUDGET, 1, 0)
    for i in range(NZ):
        st = zr_st[i]
        if NEGATIVE[i] % 2 == 1:
            st = pltpu.roll(st, HD // 2, 1)
        lse.append(st[0:1])
        largest.append(st[1:2])
    top = functools.reduce(jnp.maximum, lse)
    w = [jnp.exp2(v - top) for v in lse]
    total = functools.reduce(jnp.add, w)
    cols = turned([a * (b * (1.0 / CODE)) for a, b in zip(w, largest)] + [total, top])[:ROWS]
    o = jnp.zeros((ROWS, HD), F32)
    for i in range(NZ):
        o = o + zr_code[i].astype(I32).astype(F32) * column(cols, i)
    prompt_sum, prompt_max = column(cols, NZ), column(cols, NZ + 1)
    suffix_max = suf_m[...]
    both = jnp.maximum(prompt_max, suffix_max)
    first, second = jnp.exp2(prompt_max - both), jnp.exp2(suffix_max - both)
    denom = prompt_sum * first + suf_l[...] * second
    out_rows[...] = (o * first + suf_o[...] * second) / denom
    for h in range(GROUP):
        att_ref[:, h * HD : (h + 1) * HD] = out_rows[pl.ds(h, PART, stride=GROUP), :].astype(BF16)

    for pos in range(1, NZ):
        agz_out(pos).wait_send()
        for c in z_out(pos):
            c.wait_send()
    for j in (1, 2, 3):
        for part in range(3):
            agx_out(part, j).wait_send()
    for n in range(6):
        for c in rsx_out(n):
            c.wait_send()
    for c in window:
        c.wait()
    for c in infos:
        c.wait_send()
    finish_halo()


def halo_kernel(k_hbm, v_hbm, lowk, lowv, highk, highv, send, recv):
    me = lax.axis_index("seq")
    owners = NX * NZ
    above, below = (me + 1) % owners, (me + owners - 1) % owners
    pieces = k_hbm.shape[0] // PART
    barrier = pltpu.get_barrier_semaphore()
    for p in (above, below):
        pl.semaphore_signal(barrier, inc=1, device_id={"seq": p}, device_id_type=MESH)
    pl.semaphore_wait(barrier, 2)
    copies = [
        pltpu.make_async_remote_copy(
            src.at[pl.ds(at * pieces, HALO * pieces)],
            dst,
            send.at[i],
            recv.at[i],
            device_id={"seq": device},
            device_id_type=MESH,
        )
        for i, (src, at, dst, device) in enumerate(
            (
                (k_hbm, PART - HALO, lowk, above),
                (v_hbm, PART - HALO, lowv, above),
                (k_hbm, 0, highk, below),
                (v_hbm, 0, highv, below),
            )
        )
    ]
    for c in copies:
        c.start()
    for c in copies:
        c.wait()


def resample_kernel(
    packed,
    plan_ref,
    att_in,
    k_in,
    v_in,
    lowk,
    lowv,
    highk,
    highv,
    att_ref,
    nk_hbm,
    nv_hbm,
    buf,
    sem,
):
    pieces = k_in.shape[0] // PART
    att = pltpu.make_async_copy(att_in, att_ref, sem.at[2 * PART])
    att.start()
    outs = (nk_hbm, nv_hbm)

    def copy(src, begin, out, to, count, i):
        pltpu.make_async_copy(
            src.at[pl.ds(begin, count)], out.at[pl.ds(to, count)], sem.at[i]
        ).start()

    def whole(q, srcs, place):
        for kind in range(2):
            limit = srcs[kind].shape[0] // pieces - 1
            begin = jnp.minimum(jnp.maximum(place, 0), limit) * pieces
            copy(srcs[kind], begin, outs[kind], q * pieces, pieces, 2 * q + kind)

    def unpack(q, srcs, begin, live):
        live = jnp.minimum(jnp.maximum(live, 1), pieces)
        limit = srcs[0].shape[0] - pieces
        begin = jnp.minimum(jnp.maximum(begin, 0), limit)
        for kind in range(2):
            buf[2 * q + kind] = jnp.zeros(buf.shape[1:], BF16)

        def body(n, _):
            for kind in range(2):
                buf[2 * q + kind, n] = srcs[kind][begin + n]
            return 0

        lax.fori_loop(0, live, body, 0)
        for kind in range(2):
            i = 2 * q + kind
            copy(buf.at[i], 0, outs[kind], q * pieces, pieces, i)

    for q in range(PART):
        side, place = plan_ref[q], plan_ref[PART + q]
        begin, live = plan_ref[2 * PART + q], plan_ref[3 * PART + q]

        @pl.when(side == 0)
        def _():
            whole(q, (k_in, v_in), place)

        for n, srcs in ((1, (lowk, lowv)), (2, (highk, highv))):

            @pl.when(side == n)
            def _():
                if packed:
                    unpack(q, srcs, begin, live)
                else:
                    whole(q, srcs, place)

    for q in range(PART):
        for kind in range(2):
            rows = pl.ds(q * pieces, pieces)
            pltpu.make_async_copy(buf.at[0], outs[kind].at[rows], sem.at[2 * q + kind]).wait()
    att.wait()


def on_device(
    queries,
    prompt_keys,
    prompt_values,
    suffix_keys,
    suffix_values,
    new_keys,
    new_values,
    suffix_len,
    ancestors,
):
    slots, keys = suffix_keys.shape[1], prompt_keys.shape[0]
    q = queries.reshape(ROWS, HD)
    k, v = prompt_keys.reshape(keys, HD), prompt_values.reshape(keys, HD)
    sk = suffix_keys.reshape(PART * slots // CUT, CUT, HD)
    sv = suffix_values.reshape(PART * slots // CUT, CUT, HD)
    nk, nv = new_keys.reshape(PART, HD), new_values.reshape(PART, HD)
    hbm, vmem, smem = (
        pl.BlockSpec(memory_space=pltpu.HBM),
        pl.BlockSpec(memory_space=pltpu.VMEM),
        pl.BlockSpec(memory_space=pltpu.SMEM),
    )
    shape = jax.ShapeDtypeStruct
    window = shape((PART * slots // CUT, CUT, HD), BF16)
    side = shape((BUDGET + slots // CUT, CUT, HD), BF16)
    dma = pltpu.SemaphoreType.DMA
    att, wk, wv, lowk, lowv, highk, highv, plan, fits = pl.pallas_call(
        attention_kernel,
        out_shape=(
            shape((PART, GROUP * HD), BF16),
            window,
            window,
            side,
            side,
            side,
            side,
            shape((4 * PART,), I32),
            shape((1,), I32),
        ),
        in_specs=[hbm] * 9,
        out_specs=(vmem, hbm, hbm, hbm, hbm, hbm, hbm, smem, smem),
        scratch_shapes=[
            pltpu.VMEM((TILES * TILE, HD), BF16),
            pltpu.VMEM((keys, HD), BF16),
            pltpu.VMEM((keys, 2 * HD), BF16),
            pltpu.VMEM((PART * slots // CUT, CUT, HD), BF16),
            pltpu.VMEM((PART * slots // CUT, CUT, HD), BF16),
            pltpu.VMEM((PART, HD), BF16),
            pltpu.VMEM((PART, HD), BF16),
            pltpu.VMEM((2 * PART, HD), F32),
            pltpu.SMEM((PART,), I32),
            pltpu.SMEM((PART,), I32),
            pltpu.VMEM((PART, HD), I32),
            pltpu.VMEM((PART, HD), I32),
            pltpu.VMEM((PART, HD), I32),
            pltpu.SMEM((PART, HD), I32),
            pltpu.SMEM((PART, HD), I32),
            pltpu.VMEM((BUDGET, CUT, HD), BF16),
            pltpu.VMEM((BUDGET, CUT, HD), BF16),
            pltpu.VMEM((BUDGET, CUT, HD), BF16),
            pltpu.VMEM((BUDGET, CUT, HD), BF16),
            pltpu.VMEM((CROSS // 2, CUT, HD), BF16),
            pltpu.VMEM((CROSS // 2, CUT, HD), BF16),
            pltpu.VMEM((TILE, keys), F32),
            pltpu.VMEM((TILE, keys), F32),
            pltpu.VMEM((TILE, HD), F32),
            pltpu.VMEM((TILE, HD), F32),
            pltpu.VMEM((TILE, 2 * HD), F32),
            pltpu.VMEM((ROWS, HD), F32),
            pltpu.VMEM((ROWS, HD), F32),
            pltpu.VMEM((ROWS, HD), F32),
            pltpu.VMEM((2 * TILE, HD), F32),
            pltpu.VMEM((2, TILE // 16, HD), F32),
            pltpu.VMEM((6, TILE, HD), I16),
            pltpu.VMEM((6, TILE // 16, HD), F32),
            pltpu.VMEM((6, TILE, HD), I16),
            pltpu.VMEM((6, TILE // 16, HD), F32),
            pltpu.VMEM((2 * TILE, HD), I16),
            pltpu.VMEM((4, 8, HD), F32),
            pltpu.VMEM((NZ, ROWS, HD), I16),
            pltpu.VMEM((NZ, 8, HD), F32),
            pltpu.VMEM((ROWS, HD), F32),
            dma((9,)),
            dma((2,)),
            dma((NZ - 1,)),
            dma((NZ - 1,)),
            dma((3, 3)),
            dma((3, 3)),
            dma((6, 2)),
            dma((6, 2)),
            dma((NZ - 1, 2)),
            dma((NZ - 1, 2)),
            dma((2,)),
            dma((2,)),
            dma((2,)),
            dma((PACKETS, 4)),
            dma((PACKETS, 4)),
            dma((3, 2)),
            dma((3, 2)),
        ],
        compiler_params=pltpu.CompilerParams(
            collective_id=0, has_side_effects=True, vmem_limit_bytes=VMEM_LIMIT
        ),
        name="attention",
    )(q, k, v, sk, sv, nk, nv, suffix_len, ancestors)

    def resample(packed, *operands):
        return pl.pallas_call(
            functools.partial(resample_kernel, packed),
            out_shape=(
                shape((PART, GROUP * HD), BF16),
                window,
                window,
            ),
            in_specs=[smem] + [hbm] * 3 + [vmem if packed else hbm] * 4,
            out_specs=(hbm, hbm, hbm),
            scratch_shapes=[
                pltpu.VMEM((2 * PART, slots // CUT, CUT, HD), BF16),
                dma((2 * PART + 1,)),
            ],
            compiler_params=pltpu.CompilerParams(vmem_limit_bytes=VMEM_LIMIT),
            name="resample",
        )(*operands)

    def whole(plan, att, wk, wv, *_):
        full = shape((HALO * slots // CUT, CUT, HD), BF16)
        sides = pl.pallas_call(
            halo_kernel,
            out_shape=(full,) * 4,
            in_specs=[hbm] * 2,
            out_specs=(hbm,) * 4,
            scratch_shapes=[dma((4,)), dma((4,))],
            compiler_params=pltpu.CompilerParams(
                collective_id=1, has_side_effects=True, vmem_limit_bytes=VMEM_LIMIT
            ),
            name="halo",
        )(wk, wv)
        return resample(False, plan, att, wk, wv, *sides)

    attended, next_keys, next_values = lax.cond(
        fits[0] > 0,
        functools.partial(resample, True),
        whole,
        plan,
        att,
        wk,
        wv,
        lowk,
        lowv,
        highk,
        highv,
    )
    return (
        attended,
        next_keys.reshape(suffix_keys.shape),
        next_values.reshape(suffix_values.shape),
    )


def solution(mesh):
    in_specs = (
        P("seq", "head", None),
        P("seq", "head", None),
        P("seq", "head", None),
        P("seq", None, "head", None),
        P("seq", None, "head", None),
        P("seq", "head", None),
        P("seq", "head", None),
        P("seq"),
        P("seq"),
    )
    out_specs = (P("seq", "head"), P("seq", None, "head", None), P("seq", None, "head", None))
    return jax.shard_map(
        on_device, mesh=mesh, in_specs=in_specs, out_specs=out_specs, check_vma=False
    )
```

```python
import functools
import math

import jax
import jax.numpy as jnp
from jax import lax
from jax.experimental import pallas as pl
from jax.experimental.pallas import tpu as pltpu
from jax.sharding import PartitionSpec as P

F32, BF16, I16, I32 = jnp.float32, jnp.bfloat16, jnp.int16, jnp.int32
MESH = pl.DeviceIdType.MESH
HD = 128
GROUP = 8
PART = 8
HALO = 4
ROWS = PART * GROUP
NX, NZ = 4, 8
TILE = 256
TILES = NX * NZ * ROWS // TILE
CHUNK = 512
LOG2E = math.log2(math.e)
SCALE = LOG2E / math.sqrt(HD)
OFFSETS = (0, 1, 7, 2, 6, 3, 5, 4)
NEGATIVE = (0, 2, 1, 4, 3, 6, 5, 7)
CUT = 32
BUDGET = 44
CROSS = 34
PACKETS = 4
PACKET_AT = (-1, 0, 1, 2)
CROSS_AT = (1, 0, 2)
VMEM_LIMIT = 60 * 2**20
CODE = 32000.0


def column(rows, j):
    return rows[:, j : j + 1]


def turned(parts):
    sub = lax.broadcasted_iota(I32, (16, HD), 0)
    top = jnp.zeros((16, HD), F32)
    for j, part in enumerate(parts):
        top = jnp.where(sub == j, part, top)
    return jnp.concatenate([top, jnp.zeros((HD - 16, HD), F32)], axis=0).T


def coded(values):
    largest = jnp.maximum(jnp.max(jnp.abs(values), axis=1, keepdims=True), 1e-30)
    codes = jnp.round(values * (CODE / largest)).astype(I32).astype(I16)
    return codes, largest


def attention_kernel(
    q_hbm,
    k_hbm,
    v_hbm,
    sk_hbm,
    sv_hbm,
    nk_hbm,
    nv_hbm,
    len_hbm,
    anc_hbm,
    att_ref,
    wk_hbm,
    wv_hbm,
    lowk_hbm,
    lowv_hbm,
    highk_hbm,
    highv_hbm,
    plan_ref,
    fits_ref,
    q_all,
    k_all,
    vx,
    sk,
    sv,
    nk_ref,
    nv_ref,
    fresh,
    len_ref,
    anc_ref,
    info,
    low_info,
    high_info,
    low_at,
    high_at,
    to_above_k,
    to_above_v,
    to_below_k,
    to_below_v,
    relay_k,
    relay_v,
    s0,
    s1,
    m0,
    m1,
    acc,
    suf_o,
    suf_m,
    suf_l,
    own_o,
    own_st,
    xs_code,
    xs_st,
    xr_code,
    xr_st,
    zs_code,
    zs_st,
    zr_code,
    zr_st,
    out_rows,
    local_sem,
    win_sem,
    agz_s,
    agz_r,
    agx_s,
    agx_r,
    rsx_s,
    rsx_r,
    rsz_s,
    rsz_r,
    info_sem,
    info_s,
    info_r,
    halo_s,
    halo_r,
    cross_s,
    cross_r,
):
    me = lax.axis_index("seq")
    x, z = me // NZ, me % NZ
    owners = NX * NZ
    above, below = (me + 1) % owners, (me + owners - 1) % owners

    def z_peer(pos):
        return x * NZ + (z + OFFSETS[pos]) % NZ

    def x_peer(j):
        return ((x + j + j // 2 - 2 * (j // 3)) % NX) * NZ + z

    def back(j):
        return 3 - j + 3 * (j // 3)

    def remote(src, dst, send, recv, device):
        return pltpu.make_async_remote_copy(
            src, dst, send, recv, device_id={"seq": device}, device_id_type=MESH
        )

    partners = [z_peer(p) for p in range(1, NZ)] + [x_peer(j) for j in (1, 2, 3)] + [above, below]
    barrier = pltpu.get_barrier_semaphore()
    for p in partners:
        pl.semaphore_signal(barrier, inc=1, device_id={"seq": p}, device_id_type=MESH)

    def tile_of(j, half):
        return j if half == 0 else 4 + j % 3

    def own_rows(pos, count=1):
        return pl.ds((TILES - 1) * TILE * (pos // 4) + (pos % 4) * ROWS, count * ROWS)

    locals_ = [
        pltpu.make_async_copy(q_hbm, q_all.at[own_rows(0)], local_sem.at[0]),
        pltpu.make_async_copy(nk_hbm, nk_ref, local_sem.at[1]),
        pltpu.make_async_copy(nv_hbm, nv_ref, local_sem.at[2]),
        pltpu.make_async_copy(len_hbm, len_ref, local_sem.at[3]),
        pltpu.make_async_copy(sk_hbm, sk, local_sem.at[4]),
        pltpu.make_async_copy(sv_hbm, sv, local_sem.at[5]),
        pltpu.make_async_copy(k_hbm, k_all, local_sem.at[6]),
        pltpu.make_async_copy(v_hbm, vx.at[:, pl.ds(0, HD)], local_sem.at[7]),
        pltpu.make_async_copy(anc_hbm, anc_ref, local_sem.at[8]),
    ]
    for c in locals_:
        c.start()
    vx[:, HD:] = jnp.ones((vx.shape[0], HD), BF16)

    locals_[3].wait()
    locals_[8].wait()
    sub = lax.broadcasted_iota(I32, (PART, HD), 0)
    lane8 = lax.broadcasted_iota(I32, (PART, HD), 1)
    table = jnp.zeros((PART, HD), I32)
    for p in range(PART):
        table = jnp.where(sub == p, jnp.where(lane8 == 0, len_ref[p], anc_ref[p]), table)
    info[...] = table
    pl.semaphore_wait(barrier, len(partners))
    infos = [
        remote(info, low_info, info_s.at[0], info_r.at[0], above),
        remote(info, high_info, info_s.at[1], info_r.at[1], below),
    ]
    for c in infos:
        c.start()

    def agz_out(pos):
        return remote(
            q_hbm,
            q_all.at[own_rows(NEGATIVE[pos])],
            agz_s.at[pos - 1],
            agz_r.at[NEGATIVE[pos] - 1],
            z_peer(pos),
        )

    def agz_in(pos):
        return remote(
            q_hbm, q_all.at[own_rows(pos)], agz_s.at[pos - 1], agz_r.at[pos - 1], z_peer(pos)
        )

    parts = ((0, 1), (1, 3), (4, 4))

    def agx(part, j, slot_there):
        pos, count = parts[part]
        start = tile_of(slot_there, pos // 4) * TILE + (pos % 4) * ROWS
        src = q_hbm if part == 0 else q_all.at[own_rows(pos, count)]
        return src, q_all.at[pl.ds(start, count * ROWS)]

    def agx_out(part, j):
        src, dst = agx(part, j, back(j))
        return remote(src, dst, agx_s.at[part, j - 1], agx_r.at[part, back(j) - 1], x_peer(j))

    def agx_in(part, j):
        src, dst = agx(part, j, j)
        return remote(src, dst, agx_s.at[part, j - 1], agx_r.at[part, j - 1], x_peer(j))

    for pos in range(1, NZ):
        agz_out(pos).start()
    for j in (1, 2, 3):
        agx_out(0, j).start()

    for i in (0, 1, 2, 4, 5):
        locals_[i].wait()
    fresh[0:PART, :] = nk_ref[...].astype(F32)
    fresh[PART : 2 * PART, :] = nv_ref[...].astype(F32)
    pieces = sk.shape[0] // PART
    slots = pieces * CUT
    row = lax.broadcasted_iota(I32, (pieces, CUT, HD), 0) * CUT + lax.broadcasted_iota(
        I32, (pieces, CUT, HD), 1
    )

    def update(p):
        mine = slice(p * pieces, (p + 1) * pieces)
        for kind, cache in ((0, sk), (1, sv)):
            new = fresh[kind * PART + p : kind * PART + p + 1, :].reshape(1, 1, HD)
            kept = jnp.where(row < len_ref[p], cache[mine].astype(F32), 0.0)
            cache[mine] = jnp.where(row == len_ref[p], new, kept).astype(BF16)

    first = me * PART

    def starts(ancestors, lengths, base):
        at = [0]
        for j in range(HALO):
            wanted = functools.reduce(
                jnp.maximum, [jnp.where(ancestors(q) == base + j, 1, 0) for q in range(PART)]
            )
            at.append(at[-1] + wanted * (lengths(j) // CUT + 1))
        return at

    def pack(at, base, to_k, to_v):
        def body(i, _):
            j = sum(jnp.where(i >= at[n], 1, 0) for n in (1, 2, 3))
            begin = functools.reduce(
                jnp.maximum, [jnp.where(i >= at[n], at[n], 0) for n in (1, 2, 3)]
            )
            piece = (base + j) * pieces + jnp.minimum(i - begin, pieces - 1)
            to_k[i] = sk[piece]
            to_v[i] = sv[piece]
            return 0

        lax.fori_loop(0, BUDGET, body, 0, unroll=4)

    to_above, to_below = (to_above_k, to_above_v), (to_below_k, to_below_v)
    low, high = (lowk_hbm, lowv_hbm), (highk_hbm, highv_hbm)
    at_top, at_bottom = z == NZ - 1, z == 0

    def packet(n, up):
        rows = pl.ds(n * (BUDGET // PACKETS), BUDGET // PACKETS)
        src, dst, device = (to_above, low, above) if up else (to_below, high, below)
        i = 0 if up else 2
        return [
            remote(
                src[kind].at[rows],
                dst[kind].at[rows],
                halo_s.at[n, i + kind],
                halo_r.at[n, i + kind],
                device,
            )
            for kind in range(2)
        ]

    def cross(stage, up):
        src, dst, device = (to_above, low, above) if up else (to_below, high, below)
        near, far = pl.ds(0, CROSS // 2), pl.ds(CROSS // 2, CROSS // 2)
        relay = (relay_k, relay_v)
        along = 1 if up else 2
        out = []
        for kind in range(2):
            if stage == 0:
                ends = src[kind].at[near], dst[kind].at[near], device
            elif stage == 1:
                ends = src[kind].at[far], relay[kind], x_peer(along)
            else:
                ends = relay[kind], dst[kind].at[far], z_peer(along)
            a, b, there = ends
            out.append(remote(a, b, cross_s.at[stage, kind], cross_r.at[stage, kind], there))
        return out

    def send_halo(when):
        for n in range(PACKETS):
            for up, edge in ((True, at_top), (False, at_bottom)):

                @pl.when(jnp.logical_and(when == PACKET_AT[n], jnp.logical_not(edge)))
                def _():
                    for c in packet(n, up):
                        c.start()

        for stage in range(3):
            for up, edge in ((True, at_top), (False, at_bottom)):

                @pl.when(jnp.logical_and(when == CROSS_AT[stage], edge))
                def _():
                    if stage == 2:
                        for c in cross(1, up):
                            c.wait_recv()
                    for c in cross(stage, up):
                        c.start()

    def finish_halo():
        for up, edge in ((True, at_top), (False, at_bottom)):

            @pl.when(jnp.logical_not(edge))
            def _():
                for n in range(PACKETS):
                    for c in packet(n, up):
                        c.wait_send()
                    for c in packet(n, not up):
                        c.wait_recv()

            @pl.when(edge)
            def _():
                for stage in range(3):
                    for c in cross(stage, up):
                        c.wait_send()
                for stage in (0, 2):
                    for c in cross(stage, not up):
                        c.wait_recv()

    for pos in (1, 2, 3):
        agz_in(pos).wait_recv()
    for j in (1, 2, 3):
        agx_out(1, j).start()
    for p in range(PART):
        update(p)
    window = [
        pltpu.make_async_copy(sk, wk_hbm, win_sem.at[0]),
        pltpu.make_async_copy(sv, wv_hbm, win_sem.at[1]),
    ]
    for c in window:
        c.start()
    for c in infos:
        c.wait_recv()
    tables = [
        pltpu.make_async_copy(low_info, low_at, info_sem.at[0]),
        pltpu.make_async_copy(high_info, high_at, info_sem.at[1]),
    ]
    for c in tables:
        c.start()
    for c in tables:
        c.wait()
    pack(
        starts(lambda q: high_at[q, 1], lambda j: len_ref[PART - HALO + j], first + PART - HALO),
        PART - HALO,
        to_above_k,
        to_above_v,
    )
    pack(starts(lambda q: low_at[q, 1], lambda j: len_ref[j], first), 0, to_below_k, to_below_v)
    extra = BUDGET - CROSS
    low_row = starts(lambda q: anc_ref[q], lambda j: low_at[PART - HALO + j, 0], first - HALO)
    high_row = starts(lambda q: anc_ref[q], lambda j: high_at[j, 0], first + PART)
    need = jnp.maximum(
        low_row[-1] + jnp.where(at_bottom, extra, 0), high_row[-1] + jnp.where(at_top, extra, 0)
    ).astype(F32)

    for q in range(PART):
        local = anc_ref[q] - first
        is_low, is_high = local < 0, local >= PART
        place = jnp.where(is_low, local + HALO, jnp.where(is_high, local - PART, local))
        begin, live = local * pieces, pieces
        for j in range(HALO):
            chosen = jnp.logical_and(is_low, place == j)
            begin = jnp.where(chosen, low_row[j], begin)
            live = jnp.where(chosen, low_at[PART - HALO + j, 0] // CUT + 1, live)
            chosen = jnp.logical_and(is_high, place == j)
            begin = jnp.where(chosen, high_row[j], begin)
            live = jnp.where(chosen, high_at[j, 0] // CUT + 1, live)
        plan_ref[q] = jnp.where(is_low, 1, jnp.where(is_high, 2, 0))
        plan_ref[PART + q] = place
        plan_ref[2 * PART + q] = begin
        plan_ref[3 * PART + q] = live
    send_halo(-1)
    for pos in (4, 5, 6, 7):
        agz_in(pos).wait_recv()
    for j in (1, 2, 3):
        agx_out(2, j).start()
    for c in locals_[6:8]:
        c.wait()

    def scores(t, keys):
        q = q_all[pl.ds(pl.multiple_of(t * TILE, TILE), TILE), :]
        return lax.dot_general(
            q, k_all[keys, :], (((1,), (1,)), ((), ())), preferred_element_type=F32
        )

    n_chunks = k_all.shape[0] // CHUNK

    def step(t, s_next, m_next, s_now, m_now):
        most = None
        for c in range(n_chunks):
            keys = slice(c * CHUNK, (c + 1) * CHUNK)
            if s_next is not None:
                s = scores(t + 1, keys)
                s_next[:, keys] = s
                for g in range(CHUNK // HD):
                    part = s[:, g * HD : (g + 1) * HD]
                    most = part if most is None else jnp.maximum(most, part)
            if s_now is not None:
                top = m_now[...]
                weights = [
                    jnp.exp2(s_now[:, lo : lo + HD] * SCALE - top).astype(BF16)
                    for lo in range(c * CHUNK, (c + 1) * CHUNK, HD)
                ]
                d = jnp.dot(
                    jnp.concatenate(weights, axis=1), vx[keys, :], preferred_element_type=F32
                )
                if c == 0:
                    acc[...] = d
                else:
                    acc[...] += d
        if s_next is not None:
            m_next[...] = jnp.broadcast_to(
                jnp.max(most, axis=1, keepdims=True) * SCALE, m_next.shape
            )

    lane = lax.broadcasted_iota(I32, (TILE, HD), 1)

    def normalised(m_now):
        total = acc[:, HD:]
        return acc[:, :HD] / total, m_now[...] + jnp.log(total) * LOG2E

    def put_stats(ref, lse, largest):
        both = jnp.where(lane == 0, lse, jnp.broadcast_to(largest, lse.shape))
        one, two = [both[g * HD : (g + 1) * HD].T[:8] for g in range(TILE // HD)]
        rest = jnp.where(sub == 2, need, pltpu.roll(two, 3, 0))
        ref[...] = jnp.where(sub < 2, one, rest)

    def slot_of(n):
        return n + 1 - n // 3 * (4 - 3 * ((5 - n) // 2))

    def rsx_copies(n, i, j):
        return [
            remote(xs_code.at[n], xr_code.at[i], rsx_s.at[n, 0], rsx_r.at[i, 0], x_peer(j)),
            remote(xs_st.at[n], xr_st.at[i], rsx_s.at[n, 1], rsx_r.at[i, 1], x_peer(j)),
        ]

    def rsx_out(n):
        j = slot_of(n)
        half = n // 3
        return rsx_copies(n, 2 * (back(j) - 1) + half, j)

    def rsx_in(j, half):
        i = 2 * (j - 1) + half
        return rsx_copies(i, i, j)

    def finish_peer(t, m_now):
        n = t - 1
        o, lse = normalised(m_now)
        codes, largest = coded(o)
        xs_code[n] = codes
        put_stats(xs_st.at[n], lse, largest)
        for c in rsx_out(n):
            c.start()

    def finish_own(half, m_now):
        o, lse = normalised(m_now)
        own_o[half * TILE : (half + 1) * TILE, :] = o
        put_stats(own_st.at[half], lse, jnp.ones((TILE, 1), F32))

    def wait_tile(t):
        for n in range(6):
            j, half = (1, 2, 3, 3, 1, 2)[n], n // 3

            @pl.when(t == n + 1)
            def _():
                for part in (0, 1) if half == 0 else (2,):
                    agx_in(part, j).wait_recv()

    step(-1, s0, m0, None, None)

    def pair(i, _):
        t = 2 * i
        send_halo(i)
        wait_tile(t + 1)
        step(t, s1, m1, s0, m0)

        @pl.when(t == 0)
        def _():
            finish_own(0, m0)

        @pl.when(t > 0)
        def _():
            finish_peer(t, m0)

        wait_tile(t + 2)
        step(t + 1, s0, m0, s1, m1)
        finish_peer(t + 1, m1)
        return 0

    lax.fori_loop(0, 3, pair, 0)

    def sum_x(half):
        for j in (1, 2, 3):
            for c in rsx_in(j, half):
                c.wait_recv()
        for g in range(TILE // HD):
            rows = slice(g * HD, (g + 1) * HD)
            lse = [own_st[half, 3 * g : 3 * g + 1, :]]
            for j in range(3):
                lse.append(xr_st[2 * j + half, 3 * g : 3 * g + 1, :])
            top = functools.reduce(jnp.maximum, lse)
            w = [jnp.exp2(v - top) for v in lse]
            total = functools.reduce(jnp.add, w)
            factors = [w[0] / total]
            for j in range(3):
                largest = xr_st[2 * j + half, 3 * g + 1 : 3 * g + 2, :]
                factors.append(w[j + 1] / total * (largest * (1.0 / CODE)))
            cols = turned(factors)
            at = half * TILE + g * HD
            o = own_o[at : at + HD, :] * column(cols, 0)
            for j in range(3):
                codes = xr_code[2 * j + half, rows, :].astype(I32).astype(F32)
                o = o + codes * column(cols, j + 1)
            codes, largest = coded(o)
            zs_code[at : at + HD, :] = codes
            st = jnp.broadcast_to(largest, (HD, HD)).T[:8]
            sub8 = lax.broadcasted_iota(I32, (8, HD), 0)
            most = own_st[half, 2:3, :]
            for j in range(3):
                most = jnp.maximum(most, xr_st[2 * j + half, 2:3, :])
            st = jnp.where(sub8 == 2, most, st)
            zs_st[at // HD] = jnp.where(sub8 == 0, top + jnp.log(total) * LOG2E, st)

    def z_copies(pos, i):
        return [
            remote(
                zs_code.at[pl.ds(pos * ROWS, ROWS)],
                zr_code.at[i],
                rsz_s.at[pos - 1, 0],
                rsz_r.at[i - 1, 0],
                z_peer(pos),
            ),
            remote(
                zs_st.at[pos // 2], zr_st.at[i], rsz_s.at[pos - 1, 1], rsz_r.at[i - 1, 1], z_peer(pos)
            ),
        ]

    def z_out(pos):
        return z_copies(pos, NEGATIVE[pos])

    sum_x(0)
    for pos in (1, 2, 3):
        for c in z_out(pos):
            c.start()
    step(6, s1, m1, s0, m0)
    finish_peer(6, m0)
    step(7, None, None, s1, m1)
    finish_own(1, m1)
    sum_x(1)
    for pos in (4, 5, 6, 7):
        for c in z_out(pos):
            c.start()
    send_halo(3)

    q_own = q_all[own_rows(0), :]
    q_own32 = q_own.astype(F32)
    slot = lax.broadcasted_iota(I32, (GROUP, slots), 1)
    for p in range(PART):
        mine = slice(p * GROUP, (p + 1) * GROUP)
        some = slice(p * pieces, (p + 1) * pieces)
        own_k, own_v = sk[some].reshape(slots, HD), sv[some].reshape(slots, HD)
        s = lax.dot_general(q_own, own_k, (((1,), (1,)), ((), ())), preferred_element_type=F32)
        s = s[mine] * SCALE
        new = jnp.sum(q_own32[mine] * fresh[p : p + 1, :], axis=1, keepdims=True) * SCALE
        live = slot < len_ref[p]
        top = jnp.maximum(jnp.max(jnp.where(live, s, -1e30), axis=1, keepdims=True), new)
        w = jnp.where(live, jnp.exp2(s - top), 0.0)
        nw = jnp.exp2(new - top)
        wide = jnp.concatenate([w, jnp.zeros_like(w)], axis=0).astype(BF16)
        o = jnp.dot(wide, own_v, preferred_element_type=F32)[:GROUP]
        suf_o[mine, :] = o + nw.astype(BF16).astype(F32) * fresh[PART + p : PART + p + 1, :]
        suf_m[mine, :] = jnp.broadcast_to(top, (GROUP, HD))
        suf_l[mine, :] = jnp.broadcast_to(jnp.sum(w, axis=1, keepdims=True) + nw, (GROUP, HD))

    zr_code[0] = zs_code[0:ROWS, :]
    zr_st[0] = zs_st[0]
    for pos in range(1, NZ):
        for c in z_copies(pos, pos):
            c.wait_recv()

    lse, largest = [], []
    most = jnp.max(functools.reduce(jnp.maximum, [zr_st[i][2:3] for i in range(NZ)]))
    fits_ref[0] = jnp.where(most <= BUDGET, 1, 0)
    for i in range(NZ):
        st = zr_st[i]
        if NEGATIVE[i] % 2 == 1:
            st = pltpu.roll(st, HD // 2, 1)
        lse.append(st[0:1])
        largest.append(st[1:2])
    top = functools.reduce(jnp.maximum, lse)
    w = [jnp.exp2(v - top) for v in lse]
    total = functools.reduce(jnp.add, w)
    cols = turned([a * (b * (1.0 / CODE)) for a, b in zip(w, largest)] + [total, top])[:ROWS]
    o = jnp.zeros((ROWS, HD), F32)
    for i in range(NZ):
        o = o + zr_code[i].astype(I32).astype(F32) * column(cols, i)
    prompt_sum, prompt_max = column(cols, NZ), column(cols, NZ + 1)
    suffix_max = suf_m[...]
    both = jnp.maximum(prompt_max, suffix_max)
    first, second = jnp.exp2(prompt_max - both), jnp.exp2(suffix_max - both)
    denom = prompt_sum * first + suf_l[...] * second
    out_rows[...] = (o * first + suf_o[...] * second) / denom
    for h in range(GROUP):
        att_ref[:, h * HD : (h + 1) * HD] = out_rows[pl.ds(h, PART, stride=GROUP), :].astype(BF16)

    for pos in range(1, NZ):
        agz_out(pos).wait_send()
        for c in z_out(pos):
            c.wait_send()
    for j in (1, 2, 3):
        for part in range(3):
            agx_out(part, j).wait_send()
    for n in range(6):
        for c in rsx_out(n):
            c.wait_send()
    for c in window:
        c.wait()
    for c in infos:
        c.wait_send()
    finish_halo()


def halo_kernel(k_hbm, v_hbm, lowk, lowv, highk, highv, send, recv):
    me = lax.axis_index("seq")
    owners = NX * NZ
    above, below = (me + 1) % owners, (me + owners - 1) % owners
    pieces = k_hbm.shape[0] // PART
    barrier = pltpu.get_barrier_semaphore()
    for p in (above, below):
        pl.semaphore_signal(barrier, inc=1, device_id={"seq": p}, device_id_type=MESH)
    pl.semaphore_wait(barrier, 2)
    copies = [
        pltpu.make_async_remote_copy(
            src.at[pl.ds(at * pieces, HALO * pieces)],
            dst,
            send.at[i],
            recv.at[i],
            device_id={"seq": device},
            device_id_type=MESH,
        )
        for i, (src, at, dst, device) in enumerate(
            (
                (k_hbm, PART - HALO, lowk, above),
                (v_hbm, PART - HALO, lowv, above),
                (k_hbm, 0, highk, below),
                (v_hbm, 0, highv, below),
            )
        )
    ]
    for c in copies:
        c.start()
    for c in copies:
        c.wait()


def resample_kernel(
    packed,
    plan_ref,
    att_in,
    k_in,
    v_in,
    lowk,
    lowv,
    highk,
    highv,
    att_ref,
    nk_hbm,
    nv_hbm,
    buf,
    sem,
):
    pieces = k_in.shape[0] // PART
    att = pltpu.make_async_copy(att_in, att_ref, sem.at[2 * PART])
    att.start()
    outs = (nk_hbm, nv_hbm)

    def copy(src, begin, out, to, count, i):
        pltpu.make_async_copy(
            src.at[pl.ds(begin, count)], out.at[pl.ds(to, count)], sem.at[i]
        ).start()

    def whole(q, srcs, place):
        for kind in range(2):
            limit = srcs[kind].shape[0] // pieces - 1
            begin = jnp.minimum(jnp.maximum(place, 0), limit) * pieces
            copy(srcs[kind], begin, outs[kind], q * pieces, pieces, 2 * q + kind)

    def unpack(q, srcs, begin, live):
        live = jnp.minimum(jnp.maximum(live, 1), pieces)
        limit = srcs[0].shape[0] - pieces
        begin = jnp.minimum(jnp.maximum(begin, 0), limit)
        for kind in range(2):
            buf[2 * q + kind] = jnp.zeros(buf.shape[1:], BF16)

        def body(n, _):
            for kind in range(2):
                buf[2 * q + kind, n] = srcs[kind][begin + n]
            return 0

        lax.fori_loop(0, live, body, 0)
        for kind in range(2):
            i = 2 * q + kind
            copy(buf.at[i], 0, outs[kind], q * pieces, pieces, i)

    for q in range(PART):
        side, place = plan_ref[q], plan_ref[PART + q]
        begin, live = plan_ref[2 * PART + q], plan_ref[3 * PART + q]

        @pl.when(side == 0)
        def _():
            whole(q, (k_in, v_in), place)

        for n, srcs in ((1, (lowk, lowv)), (2, (highk, highv))):

            @pl.when(side == n)
            def _():
                if packed:
                    unpack(q, srcs, begin, live)
                else:
                    whole(q, srcs, place)

    for q in range(PART):
        for kind in range(2):
            rows = pl.ds(q * pieces, pieces)
            pltpu.make_async_copy(buf.at[0], outs[kind].at[rows], sem.at[2 * q + kind]).wait()
    att.wait()


def on_device(
    queries,
    prompt_keys,
    prompt_values,
    suffix_keys,
    suffix_values,
    new_keys,
    new_values,
    suffix_len,
    ancestors,
):
    slots, keys = suffix_keys.shape[1], prompt_keys.shape[0]
    q = queries.reshape(ROWS, HD)
    k, v = prompt_keys.reshape(keys, HD), prompt_values.reshape(keys, HD)
    sk = suffix_keys.reshape(PART * slots // CUT, CUT, HD)
    sv = suffix_values.reshape(PART * slots // CUT, CUT, HD)
    nk, nv = new_keys.reshape(PART, HD), new_values.reshape(PART, HD)
    hbm, vmem, smem = (
        pl.BlockSpec(memory_space=pltpu.HBM),
        pl.BlockSpec(memory_space=pltpu.VMEM),
        pl.BlockSpec(memory_space=pltpu.SMEM),
    )
    shape = jax.ShapeDtypeStruct
    window = shape((PART * slots // CUT, CUT, HD), BF16)
    side = shape((BUDGET + slots // CUT, CUT, HD), BF16)
    dma = pltpu.SemaphoreType.DMA
    att, wk, wv, lowk, lowv, highk, highv, plan, fits = pl.pallas_call(
        attention_kernel,
        out_shape=(
            shape((PART, GROUP * HD), BF16),
            window,
            window,
            side,
            side,
            side,
            side,
            shape((4 * PART,), I32),
            shape((1,), I32),
        ),
        in_specs=[hbm] * 9,
        out_specs=(vmem, hbm, hbm, hbm, hbm, hbm, hbm, smem, smem),
        scratch_shapes=[
            pltpu.VMEM((TILES * TILE, HD), BF16),
            pltpu.VMEM((keys, HD), BF16),
            pltpu.VMEM((keys, 2 * HD), BF16),
            pltpu.VMEM((PART * slots // CUT, CUT, HD), BF16),
            pltpu.VMEM((PART * slots // CUT, CUT, HD), BF16),
            pltpu.VMEM((PART, HD), BF16),
            pltpu.VMEM((PART, HD), BF16),
            pltpu.VMEM((2 * PART, HD), F32),
            pltpu.SMEM((PART,), I32),
            pltpu.SMEM((PART,), I32),
            pltpu.VMEM((PART, HD), I32),
            pltpu.VMEM((PART, HD), I32),
            pltpu.VMEM((PART, HD), I32),
            pltpu.SMEM((PART, HD), I32),
            pltpu.SMEM((PART, HD), I32),
            pltpu.VMEM((BUDGET, CUT, HD), BF16),
            pltpu.VMEM((BUDGET, CUT, HD), BF16),
            pltpu.VMEM((BUDGET, CUT, HD), BF16),
            pltpu.VMEM((BUDGET, CUT, HD), BF16),
            pltpu.VMEM((CROSS // 2, CUT, HD), BF16),
            pltpu.VMEM((CROSS // 2, CUT, HD), BF16),
            pltpu.VMEM((TILE, keys), F32),
            pltpu.VMEM((TILE, keys), F32),
            pltpu.VMEM((TILE, HD), F32),
            pltpu.VMEM((TILE, HD), F32),
            pltpu.VMEM((TILE, 2 * HD), F32),
            pltpu.VMEM((ROWS, HD), F32),
            pltpu.VMEM((ROWS, HD), F32),
            pltpu.VMEM((ROWS, HD), F32),
            pltpu.VMEM((2 * TILE, HD), F32),
            pltpu.VMEM((2, 8, HD), F32),
            pltpu.VMEM((6, TILE, HD), I16),
            pltpu.VMEM((6, 8, HD), F32),
            pltpu.VMEM((6, TILE, HD), I16),
            pltpu.VMEM((6, 8, HD), F32),
            pltpu.VMEM((2 * TILE, HD), I16),
            pltpu.VMEM((4, 8, HD), F32),
            pltpu.VMEM((NZ, ROWS, HD), I16),
            pltpu.VMEM((NZ, 8, HD), F32),
            pltpu.VMEM((ROWS, HD), F32),
            dma((9,)),
            dma((2,)),
            dma((NZ - 1,)),
            dma((NZ - 1,)),
            dma((3, 3)),
            dma((3, 3)),
            dma((6, 2)),
            dma((6, 2)),
            dma((NZ - 1, 2)),
            dma((NZ - 1, 2)),
            dma((2,)),
            dma((2,)),
            dma((2,)),
            dma((PACKETS, 4)),
            dma((PACKETS, 4)),
            dma((3, 2)),
            dma((3, 2)),
        ],
        compiler_params=pltpu.CompilerParams(
            collective_id=0, has_side_effects=True, vmem_limit_bytes=VMEM_LIMIT
        ),
        name="attention",
    )(q, k, v, sk, sv, nk, nv, suffix_len, ancestors)

    def resample(packed, *operands):
        return pl.pallas_call(
            functools.partial(resample_kernel, packed),
            out_shape=(
                shape((PART, GROUP * HD), BF16),
                window,
                window,
            ),
            in_specs=[smem] + [hbm] * 3 + [vmem if packed else hbm] * 4,
            out_specs=(hbm, hbm, hbm),
            scratch_shapes=[
                pltpu.VMEM((2 * PART, slots // CUT, CUT, HD), BF16),
                dma((2 * PART + 1,)),
            ],
            compiler_params=pltpu.CompilerParams(vmem_limit_bytes=VMEM_LIMIT),
            name="resample",
        )(*operands)

    def whole(plan, att, wk, wv, *_):
        full = shape((HALO * slots // CUT, CUT, HD), BF16)
        sides = pl.pallas_call(
            halo_kernel,
            out_shape=(full,) * 4,
            in_specs=[hbm] * 2,
            out_specs=(hbm,) * 4,
            scratch_shapes=[dma((4,)), dma((4,))],
            compiler_params=pltpu.CompilerParams(
                collective_id=1, has_side_effects=True, vmem_limit_bytes=VMEM_LIMIT
            ),
            name="halo",
        )(wk, wv)
        return resample(False, plan, att, wk, wv, *sides)

    attended, next_keys, next_values = lax.cond(
        fits[0] > 0,
        functools.partial(resample, True),
        whole,
        plan,
        att,
        wk,
        wv,
        lowk,
        lowv,
        highk,
        highv,
    )
    return (
        attended,
        next_keys.reshape(suffix_keys.shape),
        next_values.reshape(suffix_values.shape),
    )


def solution(mesh):
    in_specs = (
        P("seq", "head", None),
        P("seq", "head", None),
        P("seq", "head", None),
        P("seq", None, "head", None),
        P("seq", None, "head", None),
        P("seq", "head", None),
        P("seq", "head", None),
        P("seq"),
        P("seq"),
    )
    out_specs = (P("seq", "head"), P("seq", None, "head", None), P("seq", None, "head", None))
    return jax.shard_map(
        on_device, mesh=mesh, in_specs=in_specs, out_specs=out_specs, check_vma=False
    )
```
